32 devices in a mesh: dp: 16 (over z, y, core), tensor: 2 (over x).
Axes of the slice: x: 2, y: 2, z: 4, core: 2. Of those that a mesh axis runs over, the one named last changes fastest.
Arguments:
- hidden: bfloat16 [16384, 1536], P(('dp', 'tensor')), may hold values from -6 to 6
- pre_gain: float32 [2, 1536], replicated, may hold values from 0.25 to 1.75
- w_zx: bfloat16 [2, 1536, 2, 3072], P(None, 'dp', None, 'tensor'), may hold values from -0.15625 to 0.15625
- w_bc: bfloat16 [2, 1536, 256], P(None, 'dp'), may hold values from -0.15625 to 0.15625
- w_dt: bfloat16 [2, 1536, 48], P(None, 'dp', 'tensor'), may hold values from -0.15625 to 0.15625
- conv_x: float32 [2, 4, 3072], P(None, None, 'tensor'), may hold values from -3 to 3
- conv_x_bias: float32 [2, 3072], P(None, 'tensor'), may hold values from -3 to 3
- conv_bc: float32 [2, 4, 256], replicated, may hold values from -3 to 3
- conv_bc_bias: float32 [2, 256], replicated, may hold values from -3 to 3
- dt_bias: float32 [2, 48], P(None, 'tensor'), may hold values from -6 to -2
- a_log: float32 [2, 48], P(None, 'tensor'), may hold values from -1 to 2.77
- d_skip: float32 [2, 48], P(None, 'tensor'), may hold values from 0.5 to 2
- norm_gain: float32 [2, 3072], P(None, 'tensor'), may hold values from 0.25 to 1.75
- w_out: bfloat16 [2, 3072, 1536], P(None, 'tensor', 'dp'), may hold values from -0.109375 to 0.109375
- cotangent: bfloat16 [16384, 1536], P(('dp', 'tensor')), may hold values from -6 to 6
Outputs:
- hidden_out: float32 [16384, 1536], P(('dp', 'tensor'))
- grad_hidden: float32 [16384, 1536], P(('dp', 'tensor'))
- grad_pre_gain: float32 [2, 1536], replicated
- grad_w_zx: float32 [2, 1536, 2, 3072], P(None, 'dp', None, 'tensor')
- grad_w_bc: float32 [2, 1536, 256], P(None, 'dp')
- grad_w_dt: float32 [2, 1536, 48], P(None, 'dp', 'tensor')
- grad_conv_x: float32 [2, 4, 3072], P(None, None, 'tensor')
- grad_conv_x_bias: float32 [2, 3072], P(None, 'tensor')
- grad_conv_bc: float32 [2, 4, 256], replicated
- grad_conv_bc_bias: float32 [2, 256], replicated
- grad_dt_bias: float32 [2, 48], P(None, 'tensor')
- grad_a_log: float32 [2, 48], P(None, 'tensor')
- grad_d_skip: float32 [2, 48], P(None, 'tensor')
- grad_norm_gain: float32 [2, 3072], P(None, 'tensor')
- grad_w_out: float32 [2, 3072, 1536], P(None, 'tensor', 'dp')
The draws below stay inside these ranges and needn't reach their ends.
All inputs are finite; a program needn't handle non-finite values.
Results may differ from the reference program's by a relative error of at most 0.009.
Values may be sent and summed in bfloat16 or wider, within the bound.
No kernel may reach another device: no remote copies, remote signals or barrier semaphores. Data moves between devices by JAX's collectives and lax.ppermute only.
A program may use at most 320 MiB of HBM per device.

```python
import jax
import jax.numpy as jnp
from jax import lax

D = 1536
HEADS = 48
STATE = 128
HEADDIM = 64
CONV = 4
BLOCK = 256
LAYERS = 2
SEQ_LEN = 1024
INNER = 3072
TOKENS = 16384


def levels(key, extent, pieces, least, top_value):
    gain = 1.0
    for dim, parts in pieces:
        draws = jax.random.uniform(jax.random.fold_in(jax.random.fold_in(key, 6), dim), (parts,), jnp.float32, least / len(pieces), top_value / len(pieces))
        gain = gain * jnp.repeat(jnp.exp(draws), extent[dim] // parts).reshape((-1,) + (1,) * (len(extent) - 1 - dim))
    return gain


def gaussian(stream_key, dims, scale, bound, split=(), held_as=jnp.bfloat16):
    values = jax.random.normal(stream_key, dims, jnp.float32) * scale
    if len(split) > 0:
        values = levels(stream_key, dims, split, -0.22, 0.18) * values
    return jnp.clip(values, min=-bound, max=bound).astype(held_as)


def setup_inputs(seed: int = 0) -> dict:
    key_of = jax.random.split(jax.random.key(seed), 16)
    hidden = gaussian(key_of[0], (TOKENS, D), 1.0, 6.0, ((0, 32),))
    pre_gain = jnp.clip(1.0 + 0.15 * jax.random.normal(key_of[1], (LAYERS, D), jnp.float32), 0.25, 1.75)
    w_zx = gaussian(key_of[2], (LAYERS, D, 2, INNER), D ** -0.5, 0.15625, ((1, 16), (3, 2)))
    w_bc = gaussian(key_of[3], (LAYERS, D, 2 * STATE), D ** -0.5, 0.15625, ((1, 16),))
    w_dt = gaussian(key_of[4], (LAYERS, D, HEADS), D ** -0.5, 0.15625, ((1, 16), (2, 2)))
    conv_x = gaussian(key_of[5], (LAYERS, CONV, INNER), CONV ** -0.5, 3.0, ((2, 2),), jnp.float32)
    conv_x_bias = gaussian(key_of[6], (LAYERS, INNER), 0.5, 3.0, ((1, 2),), jnp.float32)
    conv_bc = gaussian(key_of[7], (LAYERS, CONV, 2 * STATE), CONV ** -0.5, 3.0, (), jnp.float32)
    conv_bc_bias = gaussian(key_of[8], (LAYERS, 2 * STATE), 0.5, 3.0, (), jnp.float32)
    dt_bias = jnp.clip(-6.0 + 4.0 * jax.random.uniform(key_of[9], (LAYERS, HEADS), jnp.float32) ** levels(key_of[9], (LAYERS, HEADS), ((1, 2),), -0.2, 0.2), -6.0, -2.0)
    a_log = jnp.clip(-1.0 + 3.77 * jax.random.uniform(key_of[10], (LAYERS, HEADS), jnp.float32) ** levels(key_of[10], (LAYERS, HEADS), ((1, 2),), -0.2, 0.2), -1.0, 2.77)
    d_skip = jnp.clip(0.5 + 1.5 * jax.random.uniform(key_of[11], (LAYERS, HEADS), jnp.float32) ** levels(key_of[11], (LAYERS, HEADS), ((1, 2),), -0.2, 0.2), 0.5, 2.0)
    norm_gain = jnp.clip(1.0 + 0.15 * jax.random.normal(key_of[12], (LAYERS, INNER), jnp.float32), 0.25, 1.75)
    w_out = gaussian(key_of[13], (LAYERS, INNER, D), INNER ** -0.5, 0.109375, ((1, 2), (2, 16)))
    cotangent = gaussian(key_of[14], (TOKENS, D), 1.0, 6.0, ((0, 32),))
    return {"hidden": hidden, "pre_gain": pre_gain, "w_zx": w_zx, "w_bc": w_bc, "w_dt": w_dt, "conv_x": conv_x, "conv_x_bias": conv_x_bias, "conv_bc": conv_bc, "conv_bc_bias": conv_bc_bias, "dt_bias": dt_bias, "a_log": a_log, "d_skip": d_skip, "norm_gain": norm_gain, "w_out": w_out, "cotangent": cotangent}


epsilon = 1e-05
highest = lax.Precision.HIGHEST

@jax.custom_vjp
def low(v):
    return lax.optimization_barrier(v.astype(jnp.bfloat16)).astype(jnp.float32)

@jax.custom_vjp
def low_back(v):
    return v

def low_keep(v):
    return (low(v), None)

def low_pass(kept, grad):
    return (grad,)

def back_keep(v):
    return (v, None)

def back_low(kept, grad):
    return (low(grad),)
low.defvjp(low_keep, low_pass)
low_back.defvjp(back_keep, back_low)

def causal_conv(values, taps, offset):
    tap_count = taps.shape[0]
    padded = jnp.pad(values, ((tap_count - 1, 0), (0, 0)))
    result = jnp.zeros_like(values) + offset[None, :]
    for position in range(tap_count):
        result = result + taps[position][None, :] * padded[position:position + values.shape[0]]
    return result

def ssd_block(carried_state, block_inputs):
    x_heads, step_sizes, decay_rates, b_part, c_part = block_inputs
    rows_here = x_heads.shape[0]
    cumulative = jnp.cumsum(decay_rates, axis=0)
    causal_mask = (jnp.arange(rows_here)[:, None] >= jnp.arange(rows_here)[None, :]).astype(cumulative.dtype)
    across = jnp.transpose(cumulative)
    spread = across[:, :, None] - across[:, None, :]
    kernel = jnp.exp(jnp.where(causal_mask[None] > 0.5, spread, 0.0)) * causal_mask[None]
    matches = jnp.dot(c_part, jnp.transpose(b_part), precision=highest)
    driven = x_heads * step_sizes[:, :, None]
    within = jnp.einsum('hij,jhp->ihp', kernel * matches[None], driven, precision=highest)
    carried_out = jnp.einsum('is,hps->ihp', c_part, carried_state, precision=highest) * jnp.exp(cumulative)[:, :, None]
    remaining = jnp.exp(cumulative[-1][None, :] - cumulative)
    next_state = carried_state * jnp.exp(cumulative[-1])[:, None, None] + jnp.einsum('jhp,js->hps', driven * remaining[:, :, None], b_part, precision=highest)
    return (next_state, within + carried_out)

def ssd_scan(x_heads, step_sizes, decay_rates, b_part, c_part):
    blocks = x_heads.shape[0] // BLOCK

    def split_rows(array):
        return array.reshape((blocks, BLOCK) + array.shape[1:])
    initial = jnp.zeros((x_heads.shape[1], x_heads.shape[2], b_part.shape[1]), x_heads.dtype)
    final_state, outputs = lax.scan(jax.checkpoint(ssd_block), initial, (split_rows(x_heads), split_rows(step_sizes), split_rows(decay_rates), split_rows(b_part), split_rows(c_part)))
    return outputs.reshape(x_heads.shape)

def mixer_block(gate_pre, x_pre, dt_pre, b_part, c_part, conv_taps, conv_offset, dt_offset, log_rate, skip_gain):
    x_conv = jax.nn.silu(causal_conv(x_pre, conv_taps, conv_offset))
    step_sizes = jax.nn.softplus(dt_pre + dt_offset[None, :])
    decay_rates = -step_sizes * jnp.exp(log_rate)[None, :]
    x_heads = x_conv.reshape(x_conv.shape[0], -1, HEADDIM)
    mixed = ssd_scan(x_heads, step_sizes, decay_rates, b_part, c_part)
    mixed = mixed + skip_gain[None, :, None] * x_heads
    return mixed.reshape(x_conv.shape) * jax.nn.silu(gate_pre)

def state_inputs(bc_pre, taps, offset):
    both_parts = jax.nn.silu(causal_conv(bc_pre, taps, offset))
    state_width = both_parts.shape[1] // 2
    return (both_parts[:, :state_width], both_parts[:, state_width:])

def prenorm(current, gain_row):
    return current * lax.rsqrt(lax.optimization_barrier(jnp.mean(current * current, axis=-1, keepdims=True)) + epsilon) * gain_row[None, :]

def layer_forward(current, weights):
    pre_gain, w_zx, w_bc, w_dt, conv_x, conv_x_bias, conv_bc, conv_bc_bias, dt_bias, a_log, d_skip, norm_gain, w_out = weights
    normed = low(prenorm(current, pre_gain))
    gate_x = low_back(jnp.einsum('td,dkc->tkc', normed, w_zx, precision=highest))
    bc_pre = low_back(jnp.dot(normed, w_bc, precision=highest))
    dt_pre = low_back(jnp.dot(normed, w_dt, precision=highest))
    b_part, c_part = state_inputs(bc_pre, conv_bc, conv_bc_bias)
    gated = mixer_block(gate_x[:, 0], gate_x[:, 1], dt_pre, b_part, c_part, conv_x, conv_x_bias, dt_bias, a_log, d_skip)
    shaped = low(gated * lax.rsqrt(lax.optimization_barrier(jnp.mean(gated * gated, axis=-1, keepdims=True)) + epsilon) * norm_gain[None, :])
    return current + low_back(jnp.dot(shaped, w_out, precision=highest))

def reference(hidden, pre_gain, w_zx, w_bc, w_dt, conv_x, conv_x_bias, conv_bc, conv_bc_bias, dt_bias, a_log, d_skip, norm_gain, w_out, cotangent):
    params = (pre_gain.astype(jnp.float32), w_zx.astype(jnp.float32), w_bc.astype(jnp.float32), w_dt.astype(jnp.float32), conv_x.astype(jnp.float32), conv_x_bias.astype(jnp.float32), conv_bc.astype(jnp.float32), conv_bc_bias.astype(jnp.float32), dt_bias.astype(jnp.float32), a_log.astype(jnp.float32), d_skip.astype(jnp.float32), norm_gain.astype(jnp.float32), w_out.astype(jnp.float32))
    sequence_count = TOKENS // SEQ_LEN
    group_size = max(1, min(sequence_count, 4096 // SEQ_LEN))
    group_count = sequence_count // group_size
    hidden_groups = hidden.astype(jnp.float32).reshape(group_count, group_size, SEQ_LEN, D)
    cot_groups = cotangent.astype(jnp.float32).reshape(group_count, group_size, SEQ_LEN, D)

    def forward(hidden_group, weights):

        def one_sequence(sequence_rows):
            for layer_index in range(LAYERS):
                layer_weights = tuple((weight_arg[layer_index] for weight_arg in weights))
                sequence_rows = layer_forward(sequence_rows, layer_weights)
            return sequence_rows
        return jax.vmap(one_sequence)(hidden_group)

    def group_step(totals, inputs):
        hidden_group, cot_group = inputs
        output, pullback = jax.vjp(forward, hidden_group, params)
        grad_group, grad_weights = pullback(cot_group)
        return (jax.tree.map(jnp.add, totals, grad_weights), (output, grad_group))
    initial_sums = jax.tree.map(jnp.zeros_like, params)
    totals, (outputs, grad_groups) = lax.scan(group_step, initial_sums, (hidden_groups, cot_groups))
    hidden_out = outputs.reshape(TOKENS, D)
    grad_hidden = grad_groups.reshape(TOKENS, D)
    return (hidden_out, grad_hidden, totals[0], totals[1], totals[2], totals[3], totals[4], totals[5], totals[6], totals[7], totals[8], totals[9], totals[10], totals[11], totals[12])
```

```python
import functools
import jax
import jax.numpy as jnp
from jax import lax
from jax.experimental import pallas as pl
from jax.experimental.pallas import tpu as pltpu
from jax.sharding import PartitionSpec as P

HEADDIM = 64
INNER = 3072
LANES = 128
Q = 128
GROUP = 256
LOG2E = 1.4426950408889634
epsilon = 1e-05
highest = lax.Precision.HIGHEST
bf16 = jnp.bfloat16
f32 = jnp.float32


def sigmoid(v):
    return 0.5 * jnp.tanh(0.5 * v) + 0.5


def mm(a, b, precision=None):
    return lax.dot_general(
        a, b, (((1,), (0,)), ((), ())), precision=precision, preferred_element_type=f32
    )


def mm_t(a, b):
    return lax.dot_general(a, b, (((1,), (1,)), ((), ())), preferred_element_type=f32)


def t_mm(a, b):
    return lax.dot_general(a, b, (((0,), (0,)), ((), ())), preferred_element_type=f32)


def iota2(shape, dim):
    return lax.broadcasted_iota(jnp.int32, shape, dim)


def split_lanes(v):
    high = v.astype(bf16).astype(f32)
    rest = v - high
    return (high + pltpu.roll(rest, 32, axis=1)).astype(bf16)


def taps_sum(ext_ref, taps_ref, bias_ref, columns):
    total = bias_ref[0:1, columns]
    for k in range(4):
        total = total + taps_ref[k : k + 1, columns] * ext_ref[5 + k : 5 + k + Q, columns]
    return total


def chunk_terms(bcdt_ref, bext_ref, bct_ref, bcb_ref, dtv_ref, head_count):
    bext_ref[8 : 8 + Q, :] = bcdt_ref[:, 0:256]
    z = taps_sum(bext_ref, bct_ref, bcb_ref, slice(0, 256))
    s = sigmoid(z)
    bc = z * s
    dsilu = s * (1.0 + z * (1.0 - s))
    b_part = bc[:, 0:128]
    c_part = bc[:, 128:256]
    pre = bcdt_ref[:, 256:384] + dtv_ref[0:1, :]
    live = iota2((Q, LANES), 1) < head_count
    step = jnp.where(live, jnp.maximum(pre, 0.0) + jnp.log1p(jnp.exp(-jnp.abs(pre))), 0.0)
    decay = step * dtv_ref[1:2, :]
    rows = iota2((Q, Q), 0)
    cols = iota2((Q, Q), 1)
    lower = rows >= cols
    cum = mm(lower.astype(f32), decay, highest)
    return b_part, c_part, dsilu, pre, live, step, decay, cum, lower


def fwd_kernel(
    zx_ref, bcdt_ref, taps_ref, chan_ref, bct_ref, bcb_ref, dtv_ref, spread_ref,
    sh_ref, mixed_ref, sin_ref, ssq_ref, ext_ref, bext_ref, state_ref, *, head_count,
):
    width = sh_ref.shape[1]

    @pl.when(pl.program_id(0) == 0)
    def _():
        ext_ref[0:8, :] = jnp.zeros((8, width), f32)
        bext_ref[0:8, :] = jnp.zeros((8, 256), f32)
        state_ref[...] = jnp.zeros_like(state_ref)

    @pl.when(pl.program_id(0) > 0)
    def _():
        ext_ref[0:8, :] = ext_ref[Q : Q + 8, :]
        bext_ref[0:8, :] = bext_ref[Q : Q + 8, :]

    b_part, c_part, _, _, live, step, decay, cum, lower = chunk_terms(
        bcdt_ref, bext_ref, bct_ref, bcb_ref, dtv_ref, head_count
    )
    cum2 = cum * LOG2E
    across = cum2.T
    last = cum2[Q - 1 : Q, :]
    bb = b_part.astype(bf16)
    cb = c_part.astype(bf16)
    bt = b_part.T.astype(bf16)
    c_both = jnp.concatenate([cb, (c_part - cb.astype(f32)).astype(bf16)], axis=1)
    scores = jnp.where(lower, mm(c_part, b_part.T, highest), 0.0)
    step_l = split_lanes(step)
    grow_l = split_lanes(jnp.where(live, jnp.exp2(cum2), 0.0))
    left_l = split_lanes(jnp.where(live, jnp.exp2(last - cum2), 0.0))
    all_l = split_lanes(jnp.where(live[0:8], jnp.exp2(jnp.broadcast_to(last, (8, LANES))), 0.0))
    half = iota2((Q, LANES), 1) < HEADDIM
    ssq = jnp.zeros((Q, LANES), f32)
    for g in range(width // GROUP):
        columns = slice(g * GROUP, (g + 1) * GROUP)
        spread = spread_ref[:, columns]
        step_e = mm(step_l, spread)
        grow_e = mm(grow_l, spread)
        left_e = mm(left_l, spread)
        all_e = mm(all_l, spread)[0:1, :]
        ext_ref[8 : 8 + Q, columns] = zx_ref[:, width + g * GROUP : width + (g + 1) * GROUP].astype(f32)
        z = taps_sum(ext_ref, taps_ref, chan_ref, columns)
        xc = z * sigmoid(z)
        v = xc * step_e
        vb = v.astype(bf16)
        vl = (v - vb.astype(f32)).astype(bf16)
        state = state_ref[:, columns]
        state_b = state.astype(bf16)
        sin_ref[0, :, columns] = state_b
        state_l = (state - state_b.astype(f32)).astype(bf16)
        y = mm(c_both, jnp.concatenate([state_b, state_b], axis=0)) + mm(cb, state_l)
        y = y * grow_e
        parts = []
        for pair in range(GROUP // LANES):
            head = (g * GROUP + pair * LANES) // HEADDIM
            lanes = slice(pair * LANES, (pair + 1) * LANES)
            vp, vq = vb[:, lanes], vl[:, lanes]
            highs, lows = [], []
            for h in (head, head + 1):
                d = cum2[:, h : h + 1] - across[h : h + 1, :]
                m = scores * jnp.exp2(-jnp.abs(d))
                mb = m.astype(bf16)
                highs.append(mb)
                lows.append((m - mb.astype(f32)).astype(bf16))
            block = [jnp.where(half, vp, 0), jnp.where(half, 0, vp)]
            block_l = [jnp.where(half, vq, 0), jnp.where(half, 0, vq)]
            parts.append(
                mm(
                    jnp.concatenate(highs + lows + highs, axis=1),
                    jnp.concatenate(block + block + block_l, axis=0),
                )
            )
        y = y + jnp.concatenate(parts, axis=1)
        state_ref[:, columns] = state * all_e + mm(bt, (v * left_e).astype(bf16))
        mixed = y + chan_ref[2:3, columns] * xc
        mixed_ref[:, columns] = mixed.astype(bf16)
        gate = zx_ref[:, columns].astype(f32)
        gated = mixed * (gate * sigmoid(gate))
        squares = gated * gated
        ssq = ssq + squares[:, 0:LANES] + squares[:, LANES : 2 * LANES]
        sh_ref[:, columns] = gated * chan_ref[1:2, columns]
    ssq_ref[...] = ssq


def bwd_kernel(
    sg_ref, zx_ref, xprev_ref, mixed_ref, sin_ref, bcdt_ref, bcprev_ref, coef_ref,
    taps_ref, chan_ref, bct_ref, bcb_ref, dtv_ref, spread_ref, gather_ref,
    low_ref, gchan_ref, gbc_ref, gdt_ref,
    ext_ref, bext_ref, dz_ref, dbz_ref, dstate_ref, colsum_ref, *, head_count,
):
    width = sg_ref.shape[1]
    step_id = pl.program_id(0)
    is_first = step_id == pl.num_programs(0) - 1

    @pl.when(step_id == 0)
    def _():
        dz_ref[Q : Q + 8, :] = jnp.zeros((8, width), f32)
        dbz_ref[Q : Q + 8, :] = jnp.zeros((8, 256), f32)
        dstate_ref[...] = jnp.zeros_like(dstate_ref)
        gchan_ref[...] = jnp.zeros_like(gchan_ref)
        gbc_ref[...] = jnp.zeros_like(gbc_ref)
        gdt_ref[...] = jnp.zeros_like(gdt_ref)
        colsum_ref[...] = jnp.zeros_like(colsum_ref)

    @pl.when(step_id > 0)
    def _():
        dz_ref[Q : Q + 8, :] = dz_ref[0:8, :]
        dbz_ref[Q : Q + 8, :] = dbz_ref[0:8, :]

    keep = jnp.where(is_first, 0.0, 1.0)
    ext_ref[0:8, :] = xprev_ref[8:16, :].astype(f32) * keep
    bext_ref[0:8, :] = bcprev_ref[:, 0:256] * keep
    b_part, c_part, bc_dsilu, dt_pre, live, step, decay, cum, lower = chunk_terms(
        bcdt_ref, bext_ref, bct_ref, bcb_ref, dtv_ref, head_count
    )
    cum2 = cum * LOG2E
    across = cum2.T
    last = cum2[Q - 1 : Q, :]
    bb = b_part.astype(bf16)
    cb = c_part.astype(bf16)
    bt = b_part.T.astype(bf16)
    ct = c_part.T.astype(bf16)
    upper = iota2((Q, Q), 0) <= iota2((Q, Q), 1)
    scores = jnp.where(lower, mm(c_part, b_part.T, highest), 0.0)
    scores_t = scores.T
    step_l = split_lanes(step)
    grow_l = split_lanes(jnp.where(live, jnp.exp2(cum2), 0.0))
    left_l = split_lanes(jnp.where(live, jnp.exp2(last - cum2), 0.0))
    all_l = split_lanes(jnp.where(live[0:8], jnp.exp2(jnp.broadcast_to(last, (8, LANES))), 0.0))
    half = iota2((Q, LANES), 1) < HEADDIM
    coef = coef_ref[:, 0:1]
    inv = coef_ref[:, 1:2]
    d_scores = jnp.zeros((Q, Q), f32)
    d_c = jnp.zeros((Q, LANES), f32)
    d_b = jnp.zeros((Q, LANES), f32)
    row_sums = jnp.zeros((Q, LANES), f32)
    red_step = jnp.zeros((Q, LANES), f32)
    red_in = jnp.zeros((Q, LANES), f32)
    red_out = jnp.zeros((Q, LANES), f32)
    red_all = jnp.zeros((8, LANES), f32)
    ones = jnp.ones((16, Q), bf16)
    pair_rows = iota2((2 * Q, LANES), 0) // Q
    pair_cols = iota2((2 * Q, LANES), 1)
    for g in range(width // GROUP):
        columns = slice(g * GROUP, (g + 1) * GROUP)
        spread = spread_ref[:, columns]
        gather = gather_ref[columns, :]
        step_e = mm(step_l, spread)
        grow_e = mm(grow_l, spread)
        left_e = mm(left_l, spread)
        all_e = mm(all_l, spread)[0:1, :]
        ext_ref[8 : 8 + Q, columns] = zx_ref[:, width + g * GROUP : width + (g + 1) * GROUP].astype(f32)
        z = taps_sum(ext_ref, taps_ref, chan_ref, columns)
        s = sigmoid(z)
        xc = z * s
        x_dsilu = s * (1.0 + z * (1.0 - s))
        gate = zx_ref[:, columns].astype(f32)
        gs = sigmoid(gate)
        act = gate * gs
        act_d = gs * (1.0 + gate * (1.0 - gs))
        mixed = mixed_ref[:, columns].astype(f32)
        gated = mixed * act
        sg = sg_ref[:, columns] * inv
        grad_gated = sg * chan_ref[1:2, columns] - gated * coef
        dy = grad_gated * act
        low_ref[:, columns] = (grad_gated * mixed * act_d).astype(bf16)
        gchan_ref[5:6, columns] += jnp.sum(sg * gated, axis=0, keepdims=True)
        gchan_ref[6:7, columns] += jnp.sum(dy * xc, axis=0, keepdims=True)
        dyb = dy.astype(bf16)
        v = xc * step_e
        vb = v.astype(bf16)
        sin = sin_ref[0, :, columns]
        ey = dy * grow_e
        eyb = ey.astype(bf16)
        inter = ey * mm(cb, sin)
        dstate = dstate_ref[:, columns]
        dstate_b = dstate.astype(bf16)
        dv_state = mm(bb, dstate_b) * left_e
        d_c = d_c + mm_t(eyb, sin)
        d_b = d_b + mm_t((v * left_e).astype(bf16), dstate_b)
        kept = jnp.sum(sin.astype(f32) * dstate, axis=0, keepdims=True) * all_e
        dstate_ref[:, columns] = dstate * all_e + mm(ct, eyb)
        parts = []
        for pair in range(GROUP // LANES):
            lanes = slice(pair * LANES, (pair + 1) * LANES)
            head = (g * GROUP + pair * LANES) // HEADDIM
            vp = vb[:, lanes]
            dp = dyb[:, lanes]
            v_block = jnp.concatenate([jnp.where(half, vp, 0), jnp.where(half, 0, vp)], axis=0)
            d_block = jnp.concatenate([jnp.where(half, dp, 0), jnp.where(half, 0, dp)], axis=0)
            dm = mm_t(dp, v_block)
            mts = []
            ws = []
            for i, h in enumerate((head, head + 1)):
                d = cum2[:, h : h + 1] - across[h : h + 1, :]
                e = jnp.exp2(-jnp.abs(d))
                dme = dm[:, i * Q : (i + 1) * Q] * e
                d_scores = d_scores + dme
                mts.append((scores_t * e).astype(bf16))
                ws.append((dme * scores).astype(bf16))
            parts.append(mm(jnp.concatenate(mts, axis=1), d_block))
            w = jnp.concatenate(ws, axis=1)
            picks = (pair_cols == head + pair_rows).astype(bf16)
            row_sums = row_sums + mm(w, picks)
            sums = mm(ones, w)
            colsum_ref[head : head + 1, :] = sums[0:1, 0:Q]
            colsum_ref[head + 1 : head + 2, :] = sums[0:1, Q : 2 * Q]
        dv = jnp.concatenate(parts, axis=1) + dv_state
        red_step = red_step + mm((dv * xc).astype(bf16), gather)
        red_in = red_in + mm(inter.astype(bf16), gather)
        red_out = red_out + mm((v * dv_state).astype(bf16), gather)
        red_all = red_all + mm(jnp.broadcast_to(kept, (8, GROUP)), gather.astype(f32), highest)
        dz = (dv * step_e + chan_ref[2:3, columns] * dy) * x_dsilu
        dz_ref[0:Q, columns] = dz
        dx = jnp.zeros((Q, GROUP), f32)
        for k in range(4):
            dx = dx + taps_ref[k : k + 1, columns] * dz_ref[3 - k : 3 - k + Q, columns]
            gchan_ref[k : k + 1, columns] += jnp.sum(
                dz * ext_ref[5 + k : 5 + k + Q, columns], axis=0, keepdims=True
            )
        gchan_ref[4:5, columns] += jnp.sum(dz, axis=0, keepdims=True)
        low_ref[:, width + g * GROUP : width + (g + 1) * GROUP] = dx.astype(bf16)
    through = row_sums - colsum_ref[...].T + red_in
    d_decay = mm(upper.astype(f32), through, highest) + mm(
        jnp.where(upper, 0.0, 1.0), red_out, highest
    ) + red_all[0:1, :]
    d_decay = jnp.where(live, d_decay, 0.0)
    d_pre = (red_step + d_decay * dtv_ref[1:2, :]) * sigmoid(dt_pre)
    d_pre = jnp.where(live, d_pre, 0.0)
    gdt_ref[0:1, :] += jnp.sum(d_pre, axis=0, keepdims=True)
    gdt_ref[1:2, :] += jnp.sum(d_decay * decay, axis=0, keepdims=True)
    low_ref[:, 2 * width + 256 : 2 * width + 384] = d_pre.astype(bf16)
    d_scores = jnp.where(lower, d_scores, 0.0)
    d_c = d_c + mm(d_scores, b_part, highest)
    d_b = d_b + mm(d_scores.T, c_part, highest)
    dbz = jnp.concatenate([d_b, d_c], axis=1) * bc_dsilu
    dbz_ref[0:Q, :] = dbz
    dbc = jnp.zeros((Q, 256), f32)
    for k in range(4):
        dbc = dbc + bct_ref[k : k + 1, :] * dbz_ref[3 - k : 3 - k + Q, :]
        gbc_ref[k : k + 1, :] += jnp.sum(
            dbz * bext_ref[5 + k : 5 + k + Q, :], axis=0, keepdims=True
        )
    gbc_ref[4:5, :] += jnp.sum(dbz, axis=0, keepdims=True)
    low_ref[:, 2 * width : 2 * width + 256] = dbc.astype(bf16)


def spread_matrix(width):
    heads = jnp.arange(width) // HEADDIM
    lanes = jnp.arange(LANES)
    return ((lanes[:, None] == heads[None, :]) | (lanes[:, None] == heads[None, :] + 32)).astype(bf16)


def gather_matrix(width):
    heads = jnp.arange(width) // HEADDIM
    return (heads[:, None] == jnp.arange(LANES)[None, :]).astype(bf16)


def whole(shape):
    return pl.BlockSpec(shape, lambda c: (0,) * len(shape))


VMEM_LIMIT = 48 * 1024 * 1024


def mixer_forward(zx, bcdt, taps, chan, bct, bcb, dtv):
    rows, width2 = zx.shape
    width = width2 // 2
    chunks = rows // Q
    return pl.pallas_call(
        functools.partial(fwd_kernel, head_count=width // HEADDIM),
        grid=(chunks,),
        in_specs=[
            pl.BlockSpec((Q, width2), lambda c: (c, 0)),
            pl.BlockSpec((Q, 384), lambda c: (c, 0)),
            whole((4, width)), whole((8, width)), whole((4, 256)), whole((1, 256)),
            whole((8, LANES)), whole((LANES, width)),
        ],
        out_specs=[
            pl.BlockSpec((Q, width), lambda c: (c, 0)),
            pl.BlockSpec((Q, width), lambda c: (c, 0)),
            pl.BlockSpec((1, LANES, width), lambda c: (c, 0, 0)),
            pl.BlockSpec((Q, LANES), lambda c: (c, 0)),
        ],
        out_shape=[
            jax.ShapeDtypeStruct((rows, width), f32),
            jax.ShapeDtypeStruct((rows, width), bf16),
            jax.ShapeDtypeStruct((chunks, LANES, width), bf16),
            jax.ShapeDtypeStruct((rows, LANES), f32),
        ],
        scratch_shapes=[
            pltpu.VMEM((Q + 8, width), f32),
            pltpu.VMEM((Q + 8, 256), f32),
            pltpu.VMEM((LANES, width), f32),
        ],
        compiler_params=pltpu.CompilerParams(
            dimension_semantics=("arbitrary",), vmem_limit_bytes=VMEM_LIMIT
        ),
        cost_estimate=pl.CostEstimate(
            flops=2 * rows * width * 3 * LANES, bytes_accessed=rows * width * 12, transcendentals=0
        ),
    )(zx, bcdt, taps, chan, bct, bcb, dtv, spread_matrix(width))


def mixer_backward(sg, zx, mixed, sin, bcdt, coef, taps, chan, bct, bcb, dtv):
    rows, width2 = zx.shape
    width = width2 // 2
    chunks = rows // Q
    last = chunks - 1
    return pl.pallas_call(
        functools.partial(bwd_kernel, head_count=width // HEADDIM),
        grid=(chunks,),
        in_specs=[
            pl.BlockSpec((Q, width), lambda c: (last - c, 0)),
            pl.BlockSpec((Q, width2), lambda c: (last - c, 0)),
            pl.BlockSpec((16, width), lambda c: (jnp.maximum((last - c) * (Q // 16) - 1, 0), 1)),
            pl.BlockSpec((Q, width), lambda c: (last - c, 0)),
            pl.BlockSpec((1, LANES, width), lambda c: (last - c, 0, 0)),
            pl.BlockSpec((Q, 384), lambda c: (last - c, 0)),
            pl.BlockSpec((8, 384), lambda c: (jnp.maximum((last - c) * (Q // 8) - 1, 0), 0)),
            pl.BlockSpec((Q, LANES), lambda c: (last - c, 0)),
            whole((4, width)), whole((8, width)), whole((4, 256)), whole((1, 256)),
            whole((8, LANES)), whole((LANES, width)), whole((width, LANES)),
        ],
        out_specs=[
            pl.BlockSpec((Q, width2 + 384), lambda c: (last - c, 0)),
            whole((8, width)), whole((8, 256)), whole((8, LANES)),
        ],
        out_shape=[
            jax.ShapeDtypeStruct((rows, width2 + 384), bf16),
            jax.ShapeDtypeStruct((8, width), f32),
            jax.ShapeDtypeStruct((8, 256), f32),
            jax.ShapeDtypeStruct((8, LANES), f32),
        ],
        scratch_shapes=[
            pltpu.VMEM((Q + 8, width), f32),
            pltpu.VMEM((Q + 8, 256), f32),
            pltpu.VMEM((Q + 8, width), f32),
            pltpu.VMEM((Q + 8, 256), f32),
            pltpu.VMEM((LANES, width), f32),
            pltpu.VMEM((LANES, LANES), f32),
        ],
        compiler_params=pltpu.CompilerParams(
            dimension_semantics=("arbitrary",), vmem_limit_bytes=VMEM_LIMIT
        ),
        cost_estimate=pl.CostEstimate(
            flops=2 * rows * width * 10 * LANES, bytes_accessed=rows * width * 20, transcendentals=0
        ),
    )(sg, zx, zx, mixed, sin, bcdt, bcdt, coef, taps, chan, bct, bcb, dtv,
      spread_matrix(width), gather_matrix(width))


def pair_swap(v):
    return lax.ppermute(v, "tensor", ((0, 1), (1, 0)))


def both_rows(own, other, first):
    return jnp.where(
        first, jnp.concatenate([own, other], axis=0), jnp.concatenate([other, own], axis=0)
    )


def sum_devices(v):
    span = 1
    size = lax.axis_size("dp")
    while span < size:
        v = v + lax.ppermute(v, "dp", [(i, i ^ span) for i in range(size)])
        span *= 2
    return v


def head_lanes(v):
    return jnp.pad(v, ((0, LANES - v.shape[0]),))


def local(
    hidden,
    pre_gain,
    w_zx,
    w_bc,
    w_dt,
    conv_x,
    conv_x_bias,
    conv_bc,
    conv_bc_bias,
    dt_bias,
    a_log,
    d_skip,
    norm_gain,
    w_out,
    cotangent,
):
    layers = pre_gain.shape[0]
    own_count, depth = hidden.shape
    rows = own_count * lax.axis_size("tensor")
    width = w_zx.shape[-1]
    heads = dt_bias.shape[-1]
    tensor_index = lax.axis_index("tensor")
    first = tensor_index == 0

    def own_half(v):
        return lax.dynamic_slice_in_dim(v, tensor_index * own_count, own_count, 0)

    def other_half(v):
        return lax.dynamic_slice_in_dim(v, (1 - tensor_index) * own_count, own_count, 0)

    def gather_pair(v):
        return both_rows(v, pair_swap(v), first)

    in_weights = []
    out_weights = []
    for l in range(layers):
        shard = jnp.concatenate(
            [
                w_zx[l].reshape(w_zx.shape[1], -1),
                w_bc[l],
                jnp.pad(w_dt[l], ((0, 0), (0, LANES - heads))),
            ],
            axis=1,
        )
        in_weights.append(lax.all_gather(shard, "dp", axis=0, tiled=True))
        out_weights.append(lax.all_gather(w_out[l].T, "dp", axis=0, tiled=True))
    params = []
    for l in range(layers):
        chan = jnp.zeros((8, width), f32)
        chan = chan.at[0].set(conv_x_bias[l]).at[1].set(norm_gain[l])
        chan = chan.at[2].set(jnp.repeat(d_skip[l], HEADDIM))
        dtv = jnp.zeros((8, LANES), f32)
        dtv = dtv.at[0].set(head_lanes(dt_bias[l])).at[1].set(head_lanes(-jnp.exp(a_log[l])))
        params.append((conv_x[l], chan, conv_bc[l], conv_bc_bias[l][None, :], dtv))

    current = hidden.astype(f32)
    cot = gather_pair(cotangent)
    saved = []
    for l in range(layers):
        w_in = in_weights[l]
        rms = lax.rsqrt(jnp.mean(current * current, axis=1, keepdims=True) + epsilon)
        normed = gather_pair((current * rms * pre_gain[l][None, :]).astype(bf16))
        zx = mm(normed, w_in[:, : 2 * width])
        bcdt = mm(normed, w_in[:, 2 * width :])
        scaled, mixed, states, squares = mixer_forward(zx, bcdt, *params[l])
        squares = jnp.sum(squares, axis=1).reshape(8, -1)
        squares = (squares + pair_swap(squares)).reshape(rows, 1)
        inv = lax.rsqrt(squares / INNER + epsilon)
        shaped = (scaled * inv).astype(bf16)
        other = mm_t(other_half(shaped), out_weights[l])
        arrived = pair_swap(other.astype(bf16))
        own = mm_t(own_half(shaped), out_weights[l])
        lifted = own + arrived.astype(f32)
        if l == layers - 1:
            own_dot = jnp.sum(own_half(cot).astype(f32) * own, axis=1, keepdims=True)
            other_dot = jnp.sum(other_half(cot).astype(f32) * other, axis=1, keepdims=True)
            dots = jnp.where(
                first,
                jnp.concatenate([own_dot, other_dot], axis=0),
                jnp.concatenate([other_dot, own_dot], axis=0),
            ).reshape(8, -1)
            last_dot = (dots + pair_swap(dots)).reshape(rows, 1)
        saved.append((current, rms, normed, zx, bcdt, shaped, mixed, states, inv, lifted))
        current = current + lifted
    hidden_out = current
    grad_rows = cotangent.astype(f32)
    outputs = [None] * layers
    packed = [None] * layers
    for l in reversed(range(layers)):
        current, rms, normed, zx, bcdt, shaped, mixed, states, inv, lifted = saved[l]
        w_in = in_weights[l]
        if l == layers - 1:
            out_grad = cot
            row_dot = last_dot
        else:
            own_grad = grad_rows.astype(bf16)
            out_grad = gather_pair(own_grad)
            own_dot = jnp.sum(own_grad.astype(f32) * lifted, axis=1).reshape(8, -1)
            row_dot = both_rows(own_dot.reshape(-1, 1), pair_swap(own_dot).reshape(-1, 1), first)
        coef = jnp.pad(
            jnp.concatenate([inv * inv * row_dot / INNER, inv], axis=1), ((0, 0), (0, LANES - 2))
        )
        shaped_grad = mm(out_grad, out_weights[l])
        grad_out = t_mm(out_grad, shaped).astype(bf16)
        low, gchan, gbc, gdt = mixer_backward(
            shaped_grad, zx, mixed, states, bcdt, coef, *params[l]
        )
        arrived = pair_swap(mm_t(other_half(low), w_in).astype(bf16))
        normed_grad = mm_t(own_half(low), w_in) + arrived.astype(f32)
        grad_in = t_mm(normed, low[:, : 2 * width]).astype(bf16)
        grad_side = t_mm(normed, low[:, 2 * width :])
        grad_out_own = lax.psum_scatter(grad_out, "dp", scatter_dimension=0, tiled=True)
        grad_in_own = lax.psum_scatter(grad_in, "dp", scatter_dimension=0, tiled=True)
        grad_side = lax.psum_scatter(grad_side, "dp", scatter_dimension=0, tiled=True)
        unit = current * rms
        weighted = normed_grad * pre_gain[l][None, :]
        grad_pre = jnp.sum(normed_grad * unit, axis=0)
        grad_rows = grad_rows + rms * (
            weighted - unit * jnp.mean(weighted * unit, axis=1, keepdims=True)
        )
        gchan = gchan.at[7].set(grad_pre)
        packed[l] = jnp.concatenate([gchan, gbc, gdt], axis=1)
        grad_in_own = grad_in_own.astype(f32)
        grad_bc = grad_side[:, :256]
        outputs[l] = (
            grad_in_own.reshape(-1, 2, width),
            grad_bc + pair_swap(grad_bc),
            grad_side[:, 256 : 256 + heads],
            grad_out_own.astype(f32).T,
        )
    small = jnp.stack(packed)
    row = lax.broadcasted_iota(jnp.int32, small.shape, 1)
    col = lax.broadcasted_iota(jnp.int32, small.shape, 2)
    shared = ((row == 7) & (col < width)) | ((col >= width) & (col < width + 256))
    small = sum_devices(small + jnp.where(shared, pair_swap(small), 0.0))
    grad_w_zx, grad_w_bc, grad_w_dt, grad_w_out = (
        jnp.stack([o[i] for o in outputs]) for i in range(4)
    )
    return (
        hidden_out,
        grad_rows,
        small[:, 7, :width],
        grad_w_zx,
        grad_w_bc,
        grad_w_dt,
        small[:, 0:4, :width],
        small[:, 4, :width],
        small[:, 0:4, width : width + 256],
        small[:, 4, width : width + 256],
        small[:, 0, width + 256 : width + 256 + heads],
        small[:, 1, width + 256 : width + 256 + heads],
        jnp.sum(small[:, 6, :width].reshape(layers, heads, HEADDIM), axis=2),
        small[:, 5, :width],
        grad_w_out,
    )


def solution(mesh):
    return jax.shard_map(
        local,
        mesh=mesh,
        in_specs=(
            P(("dp", "tensor"), None),
            P(),
            P(None, "dp", None, "tensor"),
            P(None, "dp", None),
            P(None, "dp", "tensor"),
            P(None, None, "tensor"),
            P(None, "tensor"),
            P(),
            P(),
            P(None, "tensor"),
            P(None, "tensor"),
            P(None, "tensor"),
            P(None, "tensor"),
            P(None, "tensor", "dp"),
            P(("dp", "tensor"), None),
        ),
        out_specs=(
            P(("dp", "tensor"), None),
            P(("dp", "tensor"), None),
            P(),
            P(None, "dp", None, "tensor"),
            P(None, "dp", None),
            P(None, "dp", "tensor"),
            P(None, None, "tensor"),
            P(None, "tensor"),
            P(),
            P(),
            P(None, "tensor"),
            P(None, "tensor"),
            P(None, "tensor"),
            P(None, "tensor"),
            P(None, "tensor", "dp"),
        ),
        check_vma=False,
    )
```

```python
import functools
import jax
import jax.numpy as jnp
from jax import lax
from jax.experimental import pallas as pl
from jax.experimental.pallas import tpu as pltpu
from jax.sharding import PartitionSpec as P

HEADDIM = 64
INNER = 3072
LANES = 128
Q = 128
GROUP = 256
LOG2E = 1.4426950408889634
epsilon = 1e-05
highest = lax.Precision.HIGHEST
bf16 = jnp.bfloat16
f32 = jnp.float32


def sigmoid(v):
    return 0.5 * jnp.tanh(0.5 * v) + 0.5


def mm(a, b, precision=None):
    return lax.dot_general(
        a, b, (((1,), (0,)), ((), ())), precision=precision, preferred_element_type=f32
    )


def mm_t(a, b):
    return lax.dot_general(a, b, (((1,), (1,)), ((), ())), preferred_element_type=f32)


def t_mm(a, b):
    return lax.dot_general(a, b, (((0,), (0,)), ((), ())), preferred_element_type=f32)


def iota2(shape, dim):
    return lax.broadcasted_iota(jnp.int32, shape, dim)


def split_lanes(v):
    high = v.astype(bf16).astype(f32)
    rest = v - high
    return (high + pltpu.roll(rest, 32, axis=1)).astype(bf16)


def taps_sum(ext_ref, taps_ref, bias_ref, columns):
    total = bias_ref[0:1, columns]
    for k in range(4):
        total = total + taps_ref[k : k + 1, columns] * ext_ref[5 + k : 5 + k + Q, columns]
    return total


def chunk_terms(bcdt_ref, bext_ref, bct_ref, bcb_ref, dtv_ref, head_count):
    bext_ref[8 : 8 + Q, :] = bcdt_ref[:, 0:256]
    z = taps_sum(bext_ref, bct_ref, bcb_ref, slice(0, 256))
    s = sigmoid(z)
    bc = z * s
    dsilu = s * (1.0 + z * (1.0 - s))
    b_part = bc[:, 0:128]
    c_part = bc[:, 128:256]
    pre = bcdt_ref[:, 256:384] + dtv_ref[0:1, :]
    live = iota2((Q, LANES), 1) < head_count
    step = jnp.where(live, jnp.maximum(pre, 0.0) + jnp.log1p(jnp.exp(-jnp.abs(pre))), 0.0)
    decay = step * dtv_ref[1:2, :]
    rows = iota2((Q, Q), 0)
    cols = iota2((Q, Q), 1)
    lower = rows >= cols
    cum = mm(lower.astype(f32), decay, highest)
    return b_part, c_part, dsilu, pre, live, step, decay, cum, lower


def fwd_kernel(
    zx_ref, bcdt_ref, taps_ref, chan_ref, bct_ref, bcb_ref, dtv_ref, spread_ref,
    sh_ref, mixed_ref, sin_ref, ssq_ref, ext_ref, bext_ref, state_ref, *, head_count,
):
    width = sh_ref.shape[1]

    @pl.when(pl.program_id(0) == 0)
    def _():
        ext_ref[0:8, :] = jnp.zeros((8, width), f32)
        bext_ref[0:8, :] = jnp.zeros((8, 256), f32)
        state_ref[...] = jnp.zeros_like(state_ref)

    @pl.when(pl.program_id(0) > 0)
    def _():
        ext_ref[0:8, :] = ext_ref[Q : Q + 8, :]
        bext_ref[0:8, :] = bext_ref[Q : Q + 8, :]

    b_part, c_part, _, _, live, step, decay, cum, lower = chunk_terms(
        bcdt_ref, bext_ref, bct_ref, bcb_ref, dtv_ref, head_count
    )
    cum2 = cum * LOG2E
    across = cum2.T
    last = cum2[Q - 1 : Q, :]
    bb = b_part.astype(bf16)
    cb = c_part.astype(bf16)
    bt = b_part.T.astype(bf16)
    c_both = jnp.concatenate([cb, (c_part - cb.astype(f32)).astype(bf16)], axis=1)
    scores = jnp.where(lower, mm(c_part, b_part.T, highest), 0.0)
    step_l = split_lanes(step)
    grow_l = split_lanes(jnp.where(live, jnp.exp2(cum2), 0.0))
    left_l = split_lanes(jnp.where(live, jnp.exp2(last - cum2), 0.0))
    all_l = split_lanes(jnp.where(live[0:8], jnp.exp2(jnp.broadcast_to(last, (8, LANES))), 0.0))
    half = iota2((Q, LANES), 1) < HEADDIM
    ssq = jnp.zeros((Q, LANES), f32)
    for g in range(width // GROUP):
        columns = slice(g * GROUP, (g + 1) * GROUP)
        spread = spread_ref[:, columns]
        step_e = mm(step_l, spread)
        grow_e = mm(grow_l, spread)
        left_e = mm(left_l, spread)
        all_e = mm(all_l, spread)[0:1, :]
        ext_ref[8 : 8 + Q, columns] = zx_ref[:, width + g * GROUP : width + (g + 1) * GROUP].astype(f32)
        z = taps_sum(ext_ref, taps_ref, chan_ref, columns)
        xc = z * sigmoid(z)
        v = xc * step_e
        vb = v.astype(bf16)
        vl = (v - vb.astype(f32)).astype(bf16)
        state = state_ref[:, columns]
        state_b = state.astype(bf16)
        sin_ref[0, :, columns] = state_b
        state_l = (state - state_b.astype(f32)).astype(bf16)
        y = mm(c_both, jnp.concatenate([state_b, state_b], axis=0)) + mm(cb, state_l)
        y = y * grow_e
        parts = []
        for pair in range(GROUP // LANES):
            head = (g * GROUP + pair * LANES) // HEADDIM
            lanes = slice(pair * LANES, (pair + 1) * LANES)
            vp, vq = vb[:, lanes], vl[:, lanes]
            highs, lows = [], []
            for h in (head, head + 1):
                d = cum2[:, h : h + 1] - across[h : h + 1, :]
                m = scores * jnp.exp2(-jnp.abs(d))
                mb = m.astype(bf16)
                highs.append(mb)
                lows.append((m - mb.astype(f32)).astype(bf16))
            block = [jnp.where(half, vp, 0), jnp.where(half, 0, vp)]
            block_l = [jnp.where(half, vq, 0), jnp.where(half, 0, vq)]
            parts.append(
                mm(
                    jnp.concatenate(highs + lows + highs, axis=1),
                    jnp.concatenate(block + block + block_l, axis=0),
                )
            )
        y = y + jnp.concatenate(parts, axis=1)
        state_ref[:, columns] = state * all_e + mm(bt, (v * left_e).astype(bf16))
        mixed = y + chan_ref[2:3, columns] * xc
        mixed_ref[:, columns] = mixed.astype(bf16)
        gate = zx_ref[:, columns].astype(f32)
        gated = mixed * (gate * sigmoid(gate))
        squares = gated * gated
        ssq = ssq + squares[:, 0:LANES] + squares[:, LANES : 2 * LANES]
        sh_ref[:, columns] = gated * chan_ref[1:2, columns]
    ssq_ref[...] = ssq


def bwd_kernel(
    sg_ref, zx_ref, xprev_ref, mixed_ref, sin_ref, bcdt_ref, bcprev_ref, coef_ref,
    taps_ref, chan_ref, bct_ref, bcb_ref, dtv_ref, spread_ref, gather_ref,
    low_ref, gchan_ref, gbc_ref, gdt_ref,
    ext_ref, bext_ref, dz_ref, dbz_ref, dstate_ref, colsum_ref, *, head_count,
):
    width = sg_ref.shape[1]
    step_id = pl.program_id(0)
    is_first = step_id == pl.num_programs(0) - 1

    @pl.when(step_id == 0)
    def _():
        dz_ref[Q : Q + 8, :] = jnp.zeros((8, width), f32)
        dbz_ref[Q : Q + 8, :] = jnp.zeros((8, 256), f32)
        dstate_ref[...] = jnp.zeros_like(dstate_ref)
        gchan_ref[...] = jnp.zeros_like(gchan_ref)
        gbc_ref[...] = jnp.zeros_like(gbc_ref)
        gdt_ref[...] = jnp.zeros_like(gdt_ref)
        colsum_ref[...] = jnp.zeros_like(colsum_ref)

    @pl.when(step_id > 0)
    def _():
        dz_ref[Q : Q + 8, :] = dz_ref[0:8, :]
        dbz_ref[Q : Q + 8, :] = dbz_ref[0:8, :]

    keep = jnp.where(is_first, 0.0, 1.0)
    ext_ref[0:8, :] = xprev_ref[8:16, :].astype(f32) * keep
    bext_ref[0:8, :] = bcprev_ref[:, 0:256] * keep
    b_part, c_part, bc_dsilu, dt_pre, live, step, decay, cum, lower = chunk_terms(
        bcdt_ref, bext_ref, bct_ref, bcb_ref, dtv_ref, head_count
    )
    cum2 = cum * LOG2E
    across = cum2.T
    last = cum2[Q - 1 : Q, :]
    bb = b_part.astype(bf16)
    cb = c_part.astype(bf16)
    bt = b_part.T.astype(bf16)
    ct = c_part.T.astype(bf16)
    upper = iota2((Q, Q), 0) <= iota2((Q, Q), 1)
    scores = jnp.where(lower, mm(c_part, b_part.T, highest), 0.0)
    scores_t = scores.T
    step_l = split_lanes(step)
    grow_l = split_lanes(jnp.where(live, jnp.exp2(cum2), 0.0))
    left_l = split_lanes(jnp.where(live, jnp.exp2(last - cum2), 0.0))
    all_l = split_lanes(jnp.where(live[0:8], jnp.exp2(jnp.broadcast_to(last, (8, LANES))), 0.0))
    half = iota2((Q, LANES), 1) < HEADDIM
    coef = coef_ref[:, 0:1]
    inv = coef_ref[:, 1:2]
    d_scores = jnp.zeros((Q, Q), f32)
    d_c = jnp.zeros((Q, LANES), f32)
    d_b = jnp.zeros((Q, LANES), f32)
    row_sums = jnp.zeros((Q, LANES), f32)
    red_step = jnp.zeros((Q, LANES), f32)
    red_in = jnp.zeros((Q, LANES), f32)
    red_out = jnp.zeros((Q, LANES), f32)
    red_all = jnp.zeros((8, LANES), f32)
    ones = jnp.ones((16, Q), bf16)
    pair_rows = iota2((2 * Q, LANES), 0) // Q
    pair_cols = iota2((2 * Q, LANES), 1)
    for g in range(width // GROUP):
        columns = slice(g * GROUP, (g + 1) * GROUP)
        spread = spread_ref[:, columns]
        gather = gather_ref[columns, :]
        step_e = mm(step_l, spread)
        grow_e = mm(grow_l, spread)
        left_e = mm(left_l, spread)
        all_e = mm(all_l, spread)[0:1, :]
        ext_ref[8 : 8 + Q, columns] = zx_ref[:, width + g * GROUP : width + (g + 1) * GROUP].astype(f32)
        z = taps_sum(ext_ref, taps_ref, chan_ref, columns)
        s = sigmoid(z)
        xc = z * s
        x_dsilu = s * (1.0 + z * (1.0 - s))
        gate = zx_ref[:, columns].astype(f32)
        gs = sigmoid(gate)
        act = gate * gs
        act_d = gs * (1.0 + gate * (1.0 - gs))
        mixed = mixed_ref[:, columns].astype(f32)
        gated = mixed * act
        sg = sg_ref[:, columns] * inv
        grad_gated = sg * chan_ref[1:2, columns] - gated * coef
        dy = grad_gated * act
        low_ref[:, columns] = (grad_gated * mixed * act_d).astype(bf16)
        gchan_ref[5:6, columns] += jnp.sum(sg * gated, axis=0, keepdims=True)
        gchan_ref[6:7, columns] += jnp.sum(dy * xc, axis=0, keepdims=True)
        dyb = dy.astype(bf16)
        v = xc * step_e
        vb = v.astype(bf16)
        sin = sin_ref[0, :, columns]
        ey = dy * grow_e
        eyb = ey.astype(bf16)
        inter = ey * mm(cb, sin)
        dstate = dstate_ref[:, columns]
        dstate_b = dstate.astype(bf16)
        dv_state = mm(bb, dstate_b) * left_e
        d_c = d_c + mm_t(eyb, sin)
        d_b = d_b + mm_t((v * left_e).astype(bf16), dstate_b)
        kept = jnp.sum(sin.astype(f32) * dstate, axis=0, keepdims=True) * all_e
        dstate_ref[:, columns] = dstate * all_e + mm(ct, eyb)
        parts = []
        for pair in range(GROUP // LANES):
            lanes = slice(pair * LANES, (pair + 1) * LANES)
            head = (g * GROUP + pair * LANES) // HEADDIM
            vp = vb[:, lanes]
            dp = dyb[:, lanes]
            v_block = jnp.concatenate([jnp.where(half, vp, 0), jnp.where(half, 0, vp)], axis=0)
            d_block = jnp.concatenate([jnp.where(half, dp, 0), jnp.where(half, 0, dp)], axis=0)
            dm = mm_t(dp, v_block)
            mts = []
            ws = []
            for i, h in enumerate((head, head + 1)):
                d = cum2[:, h : h + 1] - across[h : h + 1, :]
                e = jnp.exp2(-jnp.abs(d))
                dme = dm[:, i * Q : (i + 1) * Q] * e
                d_scores = d_scores + dme
                mts.append((scores_t * e).astype(bf16))
                ws.append((dme * scores).astype(bf16))
            parts.append(mm(jnp.concatenate(mts, axis=1), d_block))
            w = jnp.concatenate(ws, axis=1)
            picks = (pair_cols == head + pair_rows).astype(bf16)
            row_sums = row_sums + mm(w, picks)
            sums = mm(ones, w)
            colsum_ref[head : head + 1, :] = sums[0:1, 0:Q]
            colsum_ref[head + 1 : head + 2, :] = sums[0:1, Q : 2 * Q]
        dv = jnp.concatenate(parts, axis=1) + dv_state
        red_step = red_step + mm((dv * xc).astype(bf16), gather)
        red_in = red_in + mm(inter.astype(bf16), gather)
        red_out = red_out + mm((v * dv_state).astype(bf16), gather)
        red_all = red_all + mm(jnp.broadcast_to(kept, (8, GROUP)), gather.astype(f32), highest)
        dz = (dv * step_e + chan_ref[2:3, columns] * dy) * x_dsilu
        dz_ref[0:Q, columns] = dz
        dx = jnp.zeros((Q, GROUP), f32)
        for k in range(4):
            dx = dx + taps_ref[k : k + 1, columns] * dz_ref[3 - k : 3 - k + Q, columns]
            gchan_ref[k : k + 1, columns] += jnp.sum(
                dz * ext_ref[5 + k : 5 + k + Q, columns], axis=0, keepdims=True
            )
        gchan_ref[4:5, columns] += jnp.sum(dz, axis=0, keepdims=True)
        low_ref[:, width + g * GROUP : width + (g + 1) * GROUP] = dx.astype(bf16)
    through = row_sums - colsum_ref[...].T + red_in
    d_decay = mm(upper.astype(f32), through, highest) + mm(
        jnp.where(upper, 0.0, 1.0), red_out, highest
    ) + red_all[0:1, :]
    d_decay = jnp.where(live, d_decay, 0.0)
    d_pre = (red_step + d_decay * dtv_ref[1:2, :]) * sigmoid(dt_pre)
    d_pre = jnp.where(live, d_pre, 0.0)
    gdt_ref[0:1, :] += jnp.sum(d_pre, axis=0, keepdims=True)
    gdt_ref[1:2, :] += jnp.sum(d_decay * decay, axis=0, keepdims=True)
    low_ref[:, 2 * width + 256 : 2 * width + 384] = d_pre.astype(bf16)
    d_scores = jnp.where(lower, d_scores, 0.0)
    d_c = d_c + mm(d_scores, b_part, highest)
    d_b = d_b + mm(d_scores.T, c_part, highest)
    dbz = jnp.concatenate([d_b, d_c], axis=1) * bc_dsilu
    dbz_ref[0:Q, :] = dbz
    dbc = jnp.zeros((Q, 256), f32)
    for k in range(4):
        dbc = dbc + bct_ref[k : k + 1, :] * dbz_ref[3 - k : 3 - k + Q, :]
        gbc_ref[k : k + 1, :] += jnp.sum(
            dbz * bext_ref[5 + k : 5 + k + Q, :], axis=0, keepdims=True
        )
    gbc_ref[4:5, :] += jnp.sum(dbz, axis=0, keepdims=True)
    low_ref[:, 2 * width : 2 * width + 256] = dbc.astype(bf16)


def spread_matrix(width):
    heads = jnp.arange(width) // HEADDIM
    lanes = jnp.arange(LANES)
    return ((lanes[:, None] == heads[None, :]) | (lanes[:, None] == heads[None, :] + 32)).astype(bf16)


def gather_matrix(width):
    heads = jnp.arange(width) // HEADDIM
    return (heads[:, None] == jnp.arange(LANES)[None, :]).astype(bf16)


def whole(shape):
    return pl.BlockSpec(shape, lambda c: (0,) * len(shape))


VMEM_LIMIT = 48 * 1024 * 1024


def mixer_forward(zx, bcdt, taps, chan, bct, bcb, dtv):
    rows, width2 = zx.shape
    width = width2 // 2
    chunks = rows // Q
    return pl.pallas_call(
        functools.partial(fwd_kernel, head_count=width // HEADDIM),
        grid=(chunks,),
        in_specs=[
            pl.BlockSpec((Q, width2), lambda c: (c, 0)),
            pl.BlockSpec((Q, 384), lambda c: (c, 0)),
            whole((4, width)), whole((8, width)), whole((4, 256)), whole((1, 256)),
            whole((8, LANES)), whole((LANES, width)),
        ],
        out_specs=[
            pl.BlockSpec((Q, width), lambda c: (c, 0)),
            pl.BlockSpec((Q, width), lambda c: (c, 0)),
            pl.BlockSpec((1, LANES, width), lambda c: (c, 0, 0)),
            pl.BlockSpec((Q, LANES), lambda c: (c, 0)),
        ],
        out_shape=[
            jax.ShapeDtypeStruct((rows, width), f32),
            jax.ShapeDtypeStruct((rows, width), bf16),
            jax.ShapeDtypeStruct((chunks, LANES, width), bf16),
            jax.ShapeDtypeStruct((rows, LANES), f32),
        ],
        scratch_shapes=[
            pltpu.VMEM((Q + 8, width), f32),
            pltpu.VMEM((Q + 8, 256), f32),
            pltpu.VMEM((LANES, width), f32),
        ],
        compiler_params=pltpu.CompilerParams(
            dimension_semantics=("arbitrary",), vmem_limit_bytes=VMEM_LIMIT
        ),
        cost_estimate=pl.CostEstimate(
            flops=2 * rows * width * 3 * LANES, bytes_accessed=rows * width * 12, transcendentals=0
        ),
    )(zx, bcdt, taps, chan, bct, bcb, dtv, spread_matrix(width))


def mixer_backward(sg, zx, mixed, sin, bcdt, coef, taps, chan, bct, bcb, dtv):
    rows, width2 = zx.shape
    width = width2 // 2
    chunks = rows // Q
    last = chunks - 1
    return pl.pallas_call(
        functools.partial(bwd_kernel, head_count=width // HEADDIM),
        grid=(chunks,),
        in_specs=[
            pl.BlockSpec((Q, width), lambda c: (last - c, 0)),
            pl.BlockSpec((Q, width2), lambda c: (last - c, 0)),
            pl.BlockSpec((16, width), lambda c: (jnp.maximum((last - c) * (Q // 16) - 1, 0), 1)),
            pl.BlockSpec((Q, width), lambda c: (last - c, 0)),
            pl.BlockSpec((1, LANES, width), lambda c: (last - c, 0, 0)),
            pl.BlockSpec((Q, 384), lambda c: (last - c, 0)),
            pl.BlockSpec((8, 384), lambda c: (jnp.maximum((last - c) * (Q // 8) - 1, 0), 0)),
            pl.BlockSpec((Q, LANES), lambda c: (last - c, 0)),
            whole((4, width)), whole((8, width)), whole((4, 256)), whole((1, 256)),
            whole((8, LANES)), whole((LANES, width)), whole((width, LANES)),
        ],
        out_specs=[
            pl.BlockSpec((Q, width2 + 384), lambda c: (last - c, 0)),
            whole((8, width)), whole((8, 256)), whole((8, LANES)),
        ],
        out_shape=[
            jax.ShapeDtypeStruct((rows, width2 + 384), bf16),
            jax.ShapeDtypeStruct((8, width), f32),
            jax.ShapeDtypeStruct((8, 256), f32),
            jax.ShapeDtypeStruct((8, LANES), f32),
        ],
        scratch_shapes=[
            pltpu.VMEM((Q + 8, width), f32),
            pltpu.VMEM((Q + 8, 256), f32),
            pltpu.VMEM((Q + 8, width), f32),
            pltpu.VMEM((Q + 8, 256), f32),
            pltpu.VMEM((LANES, width), f32),
            pltpu.VMEM((LANES, LANES), f32),
        ],
        compiler_params=pltpu.CompilerParams(
            dimension_semantics=("arbitrary",), vmem_limit_bytes=VMEM_LIMIT
        ),
        cost_estimate=pl.CostEstimate(
            flops=2 * rows * width * 10 * LANES, bytes_accessed=rows * width * 20, transcendentals=0
        ),
    )(sg, zx, zx, mixed, sin, bcdt, bcdt, coef, taps, chan, bct, bcb, dtv,
      spread_matrix(width), gather_matrix(width))


def pair_swap(v):
    return lax.ppermute(v, "tensor", ((0, 1), (1, 0)))


def both_rows(own, other, first):
    return jnp.where(
        first, jnp.concatenate([own, other], axis=0), jnp.concatenate([other, own], axis=0)
    )


def dp_factors():
    size = lax.axis_size("dp")
    known = {16: (2, 2, 4), 64: (2, 4, 2, 4)}
    return known.get(size, (size,))


def after(v, other):
    return lax.optimization_barrier((v, other))[0]


def ring_scatter(arrays, marks=()):
    size = lax.axis_size("dp")
    index = lax.axis_index("dp")
    stride = 1
    state = [v.reshape((size, v.shape[0] // size) + v.shape[1:]) for v in arrays]
    for factor in dp_factors():
        place = (index // stride) % factor
        hops = []
        for i in range(size):
            here = (i // stride) % factor
            hops.append((i, i + ((here + 1) % factor - here) * stride))
        previous = None
        for n, blocks in enumerate(state):
            outer = blocks.shape[0] // factor
            parts = blocks.reshape((outer, factor) + blocks.shape[1:])

            def pick(step):
                return lax.dynamic_index_in_dim(parts, (place + step) % factor, 1, keepdims=False)

            moving = pick(factor - 1)
            if previous is not None and factor == 2 and stride > 1:
                moving = after(moving, previous)
            for step in range(factor - 1):
                if n == len(state) - 1 and stride * factor == size and step < len(marks):
                    moving = after(moving, marks[step])
                arrived = lax.ppermute(moving, "dp", hops)
                previous = arrived
                moving = arrived.astype(f32) + pick(2 * factor - 2 - step).astype(f32)
                moving = moving.astype(blocks.dtype)
            state[n] = moving
        stride *= factor
    return [b.reshape((v.shape[0] // size,) + v.shape[1:]) for b, v in zip(state, arrays)]


def sum_devices(v):
    span = 1
    size = lax.axis_size("dp")
    sums = []
    while span < size:
        v = v + lax.ppermute(v, "dp", [(i, i ^ span) for i in range(size)])
        sums.append(v)
        span *= 2
    return sums


def head_lanes(v):
    return jnp.pad(v, ((0, LANES - v.shape[0]),))


def local(
    hidden,
    pre_gain,
    w_zx,
    w_bc,
    w_dt,
    conv_x,
    conv_x_bias,
    conv_bc,
    conv_bc_bias,
    dt_bias,
    a_log,
    d_skip,
    norm_gain,
    w_out,
    cotangent,
):
    layers = pre_gain.shape[0]
    own_count, depth = hidden.shape
    rows = own_count * lax.axis_size("tensor")
    width = w_zx.shape[-1]
    heads = dt_bias.shape[-1]
    tensor_index = lax.axis_index("tensor")
    first = tensor_index == 0

    def own_half(v):
        return lax.dynamic_slice_in_dim(v, tensor_index * own_count, own_count, 0)

    def other_half(v):
        return lax.dynamic_slice_in_dim(v, (1 - tensor_index) * own_count, own_count, 0)

    def gather_pair(v):
        return both_rows(v, pair_swap(v), first)

    in_weights = []
    out_weights = []
    for l in range(layers):
        shard = jnp.concatenate(
            [
                w_zx[l].reshape(w_zx.shape[1], -1),
                w_bc[l],
                jnp.pad(w_dt[l], ((0, 0), (0, LANES - heads))),
            ],
            axis=1,
        )
        in_weights.append(lax.all_gather(shard, "dp", axis=0, tiled=True))
        out_weights.append(lax.all_gather(w_out[l].T, "dp", axis=0, tiled=True))
    params = []
    for l in range(layers):
        chan = jnp.zeros((8, width), f32)
        chan = chan.at[0].set(conv_x_bias[l]).at[1].set(norm_gain[l])
        chan = chan.at[2].set(jnp.repeat(d_skip[l], HEADDIM))
        dtv = jnp.zeros((8, LANES), f32)
        dtv = dtv.at[0].set(head_lanes(dt_bias[l])).at[1].set(head_lanes(-jnp.exp(a_log[l])))
        params.append((conv_x[l], chan, conv_bc[l], conv_bc_bias[l][None, :], dtv))

    current = hidden.astype(f32)
    saved = []
    for l in range(layers):
        w_in = in_weights[l]
        rms = lax.rsqrt(jnp.mean(current * current, axis=1, keepdims=True) + epsilon)
        own_normed = (current * rms * pre_gain[l][None, :]).astype(bf16)
        if l == 0:
            arrived = pair_swap(jnp.concatenate([own_normed, cotangent], axis=0))
            normed = both_rows(own_normed, arrived[:own_count], first)
            cot = both_rows(cotangent, arrived[own_count:], first)
        else:
            normed = gather_pair(own_normed)
        zx = mm(normed, w_in[:, : 2 * width])
        bcdt = mm(normed, w_in[:, 2 * width :])
        scaled, mixed, states, squares = mixer_forward(zx, bcdt, *params[l])
        squares = jnp.sum(squares, axis=1).reshape(8, -1)
        squares = (squares + pair_swap(squares)).reshape(rows, 1)
        inv = lax.rsqrt(squares / INNER + epsilon)
        shaped = (scaled * inv).astype(bf16)
        other = mm_t(other_half(shaped), out_weights[l])
        arrived = pair_swap(other.astype(bf16))
        own = mm_t(own_half(shaped), out_weights[l])
        lifted = own + arrived.astype(f32)
        if l == layers - 1:
            own_dot = jnp.sum(own_half(cot).astype(f32) * own, axis=1, keepdims=True)
            other_dot = jnp.sum(other_half(cot).astype(f32) * other, axis=1, keepdims=True)
            dots = jnp.where(
                first,
                jnp.concatenate([own_dot, other_dot], axis=0),
                jnp.concatenate([other_dot, own_dot], axis=0),
            ).reshape(8, -1)
            last_dot = (dots + pair_swap(dots)).reshape(rows, 1)
        saved.append((current, rms, normed, zx, bcdt, shaped, mixed, states, inv, lifted))
        current = current + lifted
    hidden_out = current
    grad_rows = cotangent.astype(f32)
    outputs = [None] * layers
    out_parts = [None] * layers
    packed = [None] * layers
    for l in reversed(range(layers)):
        current, rms, normed, zx, bcdt, shaped, mixed, states, inv, lifted = saved[l]
        w_in = in_weights[l]
        if l == layers - 1:
            out_grad = cot
            row_dot = last_dot
        else:
            own_grad = grad_rows.astype(bf16)
            out_grad = gather_pair(own_grad)
            own_dot = jnp.sum(own_grad.astype(f32) * lifted, axis=1).reshape(8, -1)
            row_dot = both_rows(own_dot.reshape(-1, 1), pair_swap(own_dot).reshape(-1, 1), first)
        coef = jnp.pad(
            jnp.concatenate([inv * inv * row_dot / INNER, inv], axis=1), ((0, 0), (0, LANES - 2))
        )
        shaped_grad = mm(out_grad, out_weights[l])
        grad_out = t_mm(out_grad, shaped).astype(bf16)
        low, gchan, gbc, gdt = mixer_backward(
            shaped_grad, zx, mixed, states, bcdt, coef, *params[l]
        )
        if l == 0 and layers > 1:
            low, done_in = lax.optimization_barrier((low, done_in))
        arrived = pair_swap(mm_t(other_half(low), w_in).astype(bf16))
        if l > 0:
            own = mm_t(own_half(low), w_in)
            grad_in = t_mm(normed, low[:, : 2 * width]).astype(bf16)
            grad_side = t_mm(normed, low[:, 2 * width :])
            done_out = lax.psum_scatter(grad_out, "dp", scatter_dimension=0, tiled=True)
            arrived, own, grad_in, grad_side, done_out = lax.optimization_barrier(
                (arrived, own, grad_in, grad_side, done_out)
            )
            grad_out_own = done_out
            done_in = lax.psum_scatter(grad_in, "dp", scatter_dimension=0, tiled=True)
            grad_side_last = grad_side
        else:
            side_done = lax.psum_scatter(
                after(grad_side_last, done_in), "dp", scatter_dimension=0, tiled=True
            )
            grad_parts = [
                t_mm(normed, low[:, i * width : (i + 1) * width]).astype(bf16) for i in range(2)
            ]
            grad_side = t_mm(normed, low[:, 2 * width :])
            own = mm_t(own_half(low), w_in)
            arrived, own, grad_parts, grad_side = lax.optimization_barrier(
                (arrived, own, grad_parts, grad_side)
            )
            grad_out_own = None
        normed_grad = own + arrived.astype(f32)
        unit = current * rms
        weighted = normed_grad * pre_gain[l][None, :]
        grad_pre = jnp.sum(normed_grad * unit, axis=0)
        grad_rows = grad_rows + rms * (
            weighted - unit * jnp.mean(weighted * unit, axis=1, keepdims=True)
        )
        gchan = gchan.at[7].set(grad_pre)
        packed[l] = jnp.concatenate([gchan, gbc, gdt], axis=1)
        out_parts[l] = grad_out_own
    small = jnp.stack(packed)
    row = lax.broadcasted_iota(jnp.int32, small.shape, 1)
    col = lax.broadcasted_iota(jnp.int32, small.shape, 2)
    shared = ((row == 7) & (col < width)) | ((col >= width) & (col < width + 256))
    sums = sum_devices(small + jnp.where(shared, pair_swap(small), 0.0))
    small = sums[-1]
    scattered = ring_scatter([grad_out] + grad_parts + [grad_side], sums[:-1])
    out_parts[0] = scattered[0]
    in_parts = [jnp.concatenate(scattered[1:3], axis=1), done_in]
    side_parts = [scattered[3], side_done]
    for l in range(layers):
        grad_bc = side_parts[l][:, :256]
        outputs[l] = (
            in_parts[l].astype(f32).reshape(-1, 2, width),
            grad_bc + pair_swap(grad_bc),
            side_parts[l][:, 256 : 256 + heads],
            out_parts[l].astype(f32).T,
        )
    grad_w_zx, grad_w_bc, grad_w_dt, grad_w_out = (
        jnp.stack([o[i] for o in outputs]) for i in range(4)
    )
    return (
        hidden_out,
        grad_rows,
        small[:, 7, :width],
        grad_w_zx,
        grad_w_bc,
        grad_w_dt,
        small[:, 0:4, :width],
        small[:, 4, :width],
        small[:, 0:4, width : width + 256],
        small[:, 4, width : width + 256],
        small[:, 0, width + 256 : width + 256 + heads],
        small[:, 1, width + 256 : width + 256 + heads],
        jnp.sum(small[:, 6, :width].reshape(layers, heads, HEADDIM), axis=2),
        small[:, 5, :width],
        grad_w_out,
    )


def solution(mesh):
    return jax.shard_map(
        local,
        mesh=mesh,
        in_specs=(
            P(("dp", "tensor"), None),
            P(),
            P(None, "dp", None, "tensor"),
            P(None, "dp", None),
            P(None, "dp", "tensor"),
            P(None, None, "tensor"),
            P(None, "tensor"),
            P(),
            P(),
            P(None, "tensor"),
            P(None, "tensor"),
            P(None, "tensor"),
            P(None, "tensor"),
            P(None, "tensor", "dp"),
            P(("dp", "tensor"), None),
        ),
        out_specs=(
            P(("dp", "tensor"), None),
            P(("dp", "tensor"), None),
            P(),
            P(None, "dp", None, "tensor"),
            P(None, "dp", None),
            P(None, "dp", "tensor"),
            P(None, None, "tensor"),
            P(None, "tensor"),
            P(),
            P(),
            P(None, "tensor"),
            P(None, "tensor"),
            P(None, "tensor"),
            P(None, "tensor"),
            P(None, "tensor", "dp"),
        ),
        check_vma=False,
    )
```

```python
import functools
import jax
import jax.numpy as jnp
from jax import lax
from jax.experimental import pallas as pl
from jax.experimental.pallas import tpu as pltpu
from jax.sharding import PartitionSpec as P

HEADDIM = 64
INNER = 3072
LANES = 128
Q = 128
GROUP = 256
LOG2E = 1.4426950408889634
epsilon = 1e-05
highest = lax.Precision.HIGHEST
bf16 = jnp.bfloat16
f32 = jnp.float32


def sigmoid(v):
    return 0.5 * jnp.tanh(0.5 * v) + 0.5


def mm(a, b, precision=None):
    return lax.dot_general(
        a, b, (((1,), (0,)), ((), ())), precision=precision, preferred_element_type=f32
    )


def mm_t(a, b):
    return lax.dot_general(a, b, (((1,), (1,)), ((), ())), preferred_element_type=f32)


def t_mm(a, b):
    return lax.dot_general(a, b, (((0,), (0,)), ((), ())), preferred_element_type=f32)


def iota2(shape, dim):
    return lax.broadcasted_iota(jnp.int32, shape, dim)


def split_lanes(v):
    high = v.astype(bf16).astype(f32)
    rest = v - high
    return (high + pltpu.roll(rest, 32, axis=1)).astype(bf16)


def taps_sum(ext_ref, taps_ref, bias_ref, columns):
    total = bias_ref[0:1, columns]
    for k in range(4):
        total = total + taps_ref[k : k + 1, columns] * ext_ref[5 + k : 5 + k + Q, columns]
    return total


def chunk_terms(bcdt_ref, bext_ref, bct_ref, bcb_ref, dtv_ref, head_count):
    bext_ref[8 : 8 + Q, :] = bcdt_ref[:, 0:256]
    z = taps_sum(bext_ref, bct_ref, bcb_ref, slice(0, 256))
    s = sigmoid(z)
    bc = z * s
    dsilu = s * (1.0 + z * (1.0 - s))
    b_part = bc[:, 0:128]
    c_part = bc[:, 128:256]
    pre = bcdt_ref[:, 256:384] + dtv_ref[0:1, :]
    live = iota2((Q, LANES), 1) < head_count
    step = jnp.where(live, jnp.maximum(pre, 0.0) + jnp.log1p(jnp.exp(-jnp.abs(pre))), 0.0)
    decay = step * dtv_ref[1:2, :]
    rows = iota2((Q, Q), 0)
    cols = iota2((Q, Q), 1)
    lower = rows >= cols
    cum = mm(lower.astype(f32), decay, highest)
    return b_part, c_part, dsilu, pre, live, step, decay, cum, lower


def fwd_kernel(
    zx_ref, bcdt_ref, taps_ref, chan_ref, bct_ref, bcb_ref, dtv_ref, spread_ref,
    sh_ref, mixed_ref, sin_ref, ssq_ref, ext_ref, bext_ref, state_ref, *, head_count,
):
    width = sh_ref.shape[1]

    @pl.when(pl.program_id(0) == 0)
    def _():
        ext_ref[0:8, :] = jnp.zeros((8, width), f32)
        bext_ref[0:8, :] = jnp.zeros((8, 256), f32)
        state_ref[...] = jnp.zeros_like(state_ref)

    @pl.when(pl.program_id(0) > 0)
    def _():
        ext_ref[0:8, :] = ext_ref[Q : Q + 8, :]
        bext_ref[0:8, :] = bext_ref[Q : Q + 8, :]

    b_part, c_part, _, _, live, step, decay, cum, lower = chunk_terms(
        bcdt_ref, bext_ref, bct_ref, bcb_ref, dtv_ref, head_count
    )
    cum2 = cum * LOG2E
    across = cum2.T
    last = cum2[Q - 1 : Q, :]
    bb = b_part.astype(bf16)
    cb = c_part.astype(bf16)
    bt = b_part.T.astype(bf16)
    c_both = jnp.concatenate([cb, (c_part - cb.astype(f32)).astype(bf16)], axis=1)
    scores = jnp.where(lower, mm(c_part, b_part.T, highest), 0.0)
    step_l = split_lanes(step)
    grow_l = split_lanes(jnp.where(live, jnp.exp2(cum2), 0.0))
    left_l = split_lanes(jnp.where(live, jnp.exp2(last - cum2), 0.0))
    all_l = split_lanes(jnp.where(live[0:8], jnp.exp2(jnp.broadcast_to(last, (8, LANES))), 0.0))
    half = iota2((Q, LANES), 1) < HEADDIM
    ssq = jnp.zeros((Q, LANES), f32)
    for g in range(width // GROUP):
        columns = slice(g * GROUP, (g + 1) * GROUP)
        spread = spread_ref[:, columns]
        step_e = mm(step_l, spread)
        grow_e = mm(grow_l, spread)
        left_e = mm(left_l, spread)
        all_e = mm(all_l, spread)[0:1, :]
        ext_ref[8 : 8 + Q, columns] = zx_ref[:, width + g * GROUP : width + (g + 1) * GROUP].astype(f32)
        z = taps_sum(ext_ref, taps_ref, chan_ref, columns)
        xc = z * sigmoid(z)
        v = xc * step_e
        vb = v.astype(bf16)
        vl = (v - vb.astype(f32)).astype(bf16)
        state = state_ref[:, columns]
        state_b = state.astype(bf16)
        sin_ref[0, :, columns] = state_b
        state_l = (state - state_b.astype(f32)).astype(bf16)
        y = mm(c_both, jnp.concatenate([state_b, state_b], axis=0)) + mm(cb, state_l)
        y = y * grow_e
        parts = []
        for pair in range(GROUP // LANES):
            head = (g * GROUP + pair * LANES) // HEADDIM
            lanes = slice(pair * LANES, (pair + 1) * LANES)
            vp, vq = vb[:, lanes], vl[:, lanes]
            highs, lows = [], []
            for h in (head, head + 1):
                d = cum2[:, h : h + 1] - across[h : h + 1, :]
                m = scores * jnp.exp2(-jnp.abs(d))
                mb = m.astype(bf16)
                highs.append(mb)
                lows.append((m - mb.astype(f32)).astype(bf16))
            block = [jnp.where(half, vp, 0), jnp.where(half, 0, vp)]
            block_l = [jnp.where(half, vq, 0), jnp.where(half, 0, vq)]
            parts.append(
                mm(
                    jnp.concatenate(highs + lows + highs, axis=1),
                    jnp.concatenate(block + block + block_l, axis=0),
                )
            )
        y = y + jnp.concatenate(parts, axis=1)
        state_ref[:, columns] = state * all_e + mm(bt, (v * left_e).astype(bf16))
        mixed = y + chan_ref[2:3, columns] * xc
        mixed_ref[:, columns] = mixed.astype(bf16)
        gate = zx_ref[:, columns].astype(f32)
        gated = mixed * (gate * sigmoid(gate))
        squares = gated * gated
        ssq = ssq + squares[:, 0:LANES] + squares[:, LANES : 2 * LANES]
        sh_ref[:, columns] = gated * chan_ref[1:2, columns]
    ssq_ref[...] = ssq


def bwd_kernel(
    sg_ref, zx_ref, xprev_ref, mixed_ref, sin_ref, bcdt_ref, bcprev_ref, coef_ref,
    taps_ref, chan_ref, bct_ref, bcb_ref, dtv_ref, spread_ref, gather_ref,
    low_ref, gchan_ref, gbc_ref, gdt_ref,
    ext_ref, bext_ref, dz_ref, dbz_ref, dstate_ref, colsum_ref, *, head_count,
):
    width = sg_ref.shape[1]
    step_id = pl.program_id(0)
    is_first = step_id == pl.num_programs(0) - 1

    @pl.when(step_id == 0)
    def _():
        dz_ref[Q : Q + 8, :] = jnp.zeros((8, width), f32)
        dbz_ref[Q : Q + 8, :] = jnp.zeros((8, 256), f32)
        dstate_ref[...] = jnp.zeros_like(dstate_ref)
        gchan_ref[...] = jnp.zeros_like(gchan_ref)
        gbc_ref[...] = jnp.zeros_like(gbc_ref)
        gdt_ref[...] = jnp.zeros_like(gdt_ref)
        colsum_ref[...] = jnp.zeros_like(colsum_ref)

    @pl.when(step_id > 0)
    def _():
        dz_ref[Q : Q + 8, :] = dz_ref[0:8, :]
        dbz_ref[Q : Q + 8, :] = dbz_ref[0:8, :]

    keep = jnp.where(is_first, 0.0, 1.0)
    ext_ref[0:8, :] = xprev_ref[8:16, :].astype(f32) * keep
    bext_ref[0:8, :] = bcprev_ref[:, 0:256] * keep
    b_part, c_part, bc_dsilu, dt_pre, live, step, decay, cum, lower = chunk_terms(
        bcdt_ref, bext_ref, bct_ref, bcb_ref, dtv_ref, head_count
    )
    cum2 = cum * LOG2E
    across = cum2.T
    last = cum2[Q - 1 : Q, :]
    bb = b_part.astype(bf16)
    cb = c_part.astype(bf16)
    bt = b_part.T.astype(bf16)
    ct = c_part.T.astype(bf16)
    upper = iota2((Q, Q), 0) <= iota2((Q, Q), 1)
    scores = jnp.where(lower, mm(c_part, b_part.T, highest), 0.0)
    scores_t = scores.T
    step_l = split_lanes(step)
    grow_l = split_lanes(jnp.where(live, jnp.exp2(cum2), 0.0))
    left_l = split_lanes(jnp.where(live, jnp.exp2(last - cum2), 0.0))
    all_l = split_lanes(jnp.where(live[0:8], jnp.exp2(jnp.broadcast_to(last, (8, LANES))), 0.0))
    half = iota2((Q, LANES), 1) < HEADDIM
    coef = coef_ref[:, 0:1]
    inv = coef_ref[:, 1:2]
    d_scores = jnp.zeros((Q, Q), f32)
    d_c = jnp.zeros((Q, LANES), f32)
    d_b = jnp.zeros((Q, LANES), f32)
    row_sums = jnp.zeros((Q, LANES), f32)
    red_step = jnp.zeros((Q, LANES), f32)
    red_in = jnp.zeros((Q, LANES), f32)
    red_out = jnp.zeros((Q, LANES), f32)
    red_all = jnp.zeros((8, LANES), f32)
    ones = jnp.ones((16, Q), bf16)
    pair_rows = iota2((2 * Q, LANES), 0) // Q
    pair_cols = iota2((2 * Q, LANES), 1)
    for g in range(width // GROUP):
        columns = slice(g * GROUP, (g + 1) * GROUP)
        spread = spread_ref[:, columns]
        gather = gather_ref[columns, :]
        step_e = mm(step_l, spread)
        grow_e = mm(grow_l, spread)
        left_e = mm(left_l, spread)
        all_e = mm(all_l, spread)[0:1, :]
        ext_ref[8 : 8 + Q, columns] = zx_ref[:, width + g * GROUP : width + (g + 1) * GROUP].astype(f32)
        z = taps_sum(ext_ref, taps_ref, chan_ref, columns)
        s = sigmoid(z)
        xc = z * s
        x_dsilu = s * (1.0 + z * (1.0 - s))
        gate = zx_ref[:, columns].astype(f32)
        gs = sigmoid(gate)
        act = gate * gs
        act_d = gs * (1.0 + gate * (1.0 - gs))
        mixed = mixed_ref[:, columns].astype(f32)
        gated = mixed * act
        sg = sg_ref[:, columns] * inv
        grad_gated = sg * chan_ref[1:2, columns] - gated * coef
        dy = grad_gated * act
        low_ref[:, columns] = (grad_gated * mixed * act_d).astype(bf16)
        gchan_ref[5:6, columns] += jnp.sum(sg * gated, axis=0, keepdims=True)
        gchan_ref[6:7, columns] += jnp.sum(dy * xc, axis=0, keepdims=True)
        dyb = dy.astype(bf16)
        v = xc * step_e
        vb = v.astype(bf16)
        sin = sin_ref[0, :, columns]
        ey = dy * grow_e
        eyb = ey.astype(bf16)
        inter = ey * mm(cb, sin)
        dstate = dstate_ref[:, columns]
        dstate_b = dstate.astype(bf16)
        dv_state = mm(bb, dstate_b) * left_e
        d_c = d_c + mm_t(eyb, sin)
        d_b = d_b + mm_t((v * left_e).astype(bf16), dstate_b)
        kept = jnp.sum(sin.astype(f32) * dstate, axis=0, keepdims=True) * all_e
        dstate_ref[:, columns] = dstate * all_e + mm(ct, eyb)
        parts = []
        for pair in range(GROUP // LANES):
            lanes = slice(pair * LANES, (pair + 1) * LANES)
            head = (g * GROUP + pair * LANES) // HEADDIM
            vp = vb[:, lanes]
            dp = dyb[:, lanes]
            v_block = jnp.concatenate([jnp.where(half, vp, 0), jnp.where(half, 0, vp)], axis=0)
            d_block = jnp.concatenate([jnp.where(half, dp, 0), jnp.where(half, 0, dp)], axis=0)
            dm = mm_t(dp, v_block)
            mts = []
            ws = []
            for i, h in enumerate((head, head + 1)):
                d = cum2[:, h : h + 1] - across[h : h + 1, :]
                e = jnp.exp2(-jnp.abs(d))
                dme = dm[:, i * Q : (i + 1) * Q] * e
                d_scores = d_scores + dme
                mts.append((scores_t * e).astype(bf16))
                ws.append((dme * scores).astype(bf16))
            parts.append(mm(jnp.concatenate(mts, axis=1), d_block))
            w = jnp.concatenate(ws, axis=1)
            picks = (pair_cols == head + pair_rows).astype(bf16)
            row_sums = row_sums + mm(w, picks)
            sums = mm(ones, w)
            colsum_ref[head : head + 1, :] = sums[0:1, 0:Q]
            colsum_ref[head + 1 : head + 2, :] = sums[0:1, Q : 2 * Q]
        dv = jnp.concatenate(parts, axis=1) + dv_state
        red_step = red_step + mm((dv * xc).astype(bf16), gather)
        red_in = red_in + mm(inter.astype(bf16), gather)
        red_out = red_out + mm((v * dv_state).astype(bf16), gather)
        red_all = red_all + mm(jnp.broadcast_to(kept, (8, GROUP)), gather.astype(f32), highest)
        dz = (dv * step_e + chan_ref[2:3, columns] * dy) * x_dsilu
        dz_ref[0:Q, columns] = dz
        dx = jnp.zeros((Q, GROUP), f32)
        for k in range(4):
            dx = dx + taps_ref[k : k + 1, columns] * dz_ref[3 - k : 3 - k + Q, columns]
            gchan_ref[k : k + 1, columns] += jnp.sum(
                dz * ext_ref[5 + k : 5 + k + Q, columns], axis=0, keepdims=True
            )
        gchan_ref[4:5, columns] += jnp.sum(dz, axis=0, keepdims=True)
        low_ref[:, width + g * GROUP : width + (g + 1) * GROUP] = dx.astype(bf16)
    through = row_sums - colsum_ref[...].T + red_in
    d_decay = mm(upper.astype(f32), through, highest) + mm(
        jnp.where(upper, 0.0, 1.0), red_out, highest
    ) + red_all[0:1, :]
    d_decay = jnp.where(live, d_decay, 0.0)
    d_pre = (red_step + d_decay * dtv_ref[1:2, :]) * sigmoid(dt_pre)
    d_pre = jnp.where(live, d_pre, 0.0)
    gdt_ref[0:1, :] += jnp.sum(d_pre, axis=0, keepdims=True)
    gdt_ref[1:2, :] += jnp.sum(d_decay * decay, axis=0, keepdims=True)
    low_ref[:, 2 * width + 256 : 2 * width + 384] = d_pre.astype(bf16)
    d_scores = jnp.where(lower, d_scores, 0.0)
    d_c = d_c + mm(d_scores, b_part, highest)
    d_b = d_b + mm(d_scores.T, c_part, highest)
    dbz = jnp.concatenate([d_b, d_c], axis=1) * bc_dsilu
    dbz_ref[0:Q, :] = dbz
    dbc = jnp.zeros((Q, 256), f32)
    for k in range(4):
        dbc = dbc + bct_ref[k : k + 1, :] * dbz_ref[3 - k : 3 - k + Q, :]
        gbc_ref[k : k + 1, :] += jnp.sum(
            dbz * bext_ref[5 + k : 5 + k + Q, :], axis=0, keepdims=True
        )
    gbc_ref[4:5, :] += jnp.sum(dbz, axis=0, keepdims=True)
    low_ref[:, 2 * width : 2 * width + 256] = dbc.astype(bf16)


def spread_matrix(width):
    heads = jnp.arange(width) // HEADDIM
    lanes = jnp.arange(LANES)
    return ((lanes[:, None] == heads[None, :]) | (lanes[:, None] == heads[None, :] + 32)).astype(bf16)


def gather_matrix(width):
    heads = jnp.arange(width) // HEADDIM
    return (heads[:, None] == jnp.arange(LANES)[None, :]).astype(bf16)


def whole(shape):
    return pl.BlockSpec(shape, lambda c: (0,) * len(shape))


VMEM_LIMIT = 48 * 1024 * 1024
LIGHT = pl.CostEstimate(flops=1000, bytes_accessed=1000, transcendentals=0)


def product_t(a, b, out_dtype, columns=512):
    rows, depth = a.shape
    count = b.shape[0]

    def body(a_ref, b_ref, o_ref):
        o_ref[...] = mm_t(a_ref[...], b_ref[...]).astype(out_dtype)

    return pl.pallas_call(
        body,
        grid=(count // columns,),
        in_specs=[
            pl.BlockSpec((rows, depth), lambda j: (0, 0)),
            pl.BlockSpec((columns, depth), lambda j: (j, 0)),
        ],
        out_specs=pl.BlockSpec((rows, columns), lambda j: (0, j)),
        out_shape=jax.ShapeDtypeStruct((rows, count), out_dtype),
        compiler_params=pltpu.CompilerParams(vmem_limit_bytes=VMEM_LIMIT),
        cost_estimate=LIGHT,
    )(a, b)


def t_product(a, b, out_dtype, first, count, columns=512):
    depth, rows = a.shape
    offset = first // columns

    def body(a_ref, b_ref, o_ref):
        o_ref[...] = t_mm(a_ref[...], b_ref[...]).astype(out_dtype)

    return pl.pallas_call(
        body,
        grid=(count // columns,),
        in_specs=[
            pl.BlockSpec((depth, rows), lambda j: (0, 0)),
            pl.BlockSpec((depth, columns), lambda j: (0, offset + j)),
        ],
        out_specs=pl.BlockSpec((rows, columns), lambda j: (0, j)),
        out_shape=jax.ShapeDtypeStruct((rows, count), out_dtype),
        compiler_params=pltpu.CompilerParams(vmem_limit_bytes=VMEM_LIMIT),
        cost_estimate=LIGHT,
    )(a, b)


def mixer_forward(zx, taps, chan, bct, bcb, dtv):
    rows = zx.shape[0]
    width2 = zx.shape[1] - 384
    width = width2 // 2
    side = width2 // 384
    chunks = rows // Q
    return pl.pallas_call(
        functools.partial(fwd_kernel, head_count=width // HEADDIM),
        grid=(chunks,),
        in_specs=[
            pl.BlockSpec((Q, width2), lambda c: (c, 0)),
            pl.BlockSpec((Q, 384), lambda c: (c, side)),
            whole((4, width)), whole((8, width)), whole((4, 256)), whole((1, 256)),
            whole((8, LANES)), whole((LANES, width)),
        ],
        out_specs=[
            pl.BlockSpec((Q, width), lambda c: (c, 0)),
            pl.BlockSpec((Q, width), lambda c: (c, 0)),
            pl.BlockSpec((1, LANES, width), lambda c: (c, 0, 0)),
            pl.BlockSpec((Q, LANES), lambda c: (c, 0)),
        ],
        out_shape=[
            jax.ShapeDtypeStruct((rows, width), f32),
            jax.ShapeDtypeStruct((rows, width), bf16),
            jax.ShapeDtypeStruct((chunks, LANES, width), bf16),
            jax.ShapeDtypeStruct((rows, LANES), f32),
        ],
        scratch_shapes=[
            pltpu.VMEM((Q + 8, width), f32),
            pltpu.VMEM((Q + 8, 256), f32),
            pltpu.VMEM((LANES, width), f32),
        ],
        compiler_params=pltpu.CompilerParams(
            dimension_semantics=("arbitrary",), vmem_limit_bytes=VMEM_LIMIT
        ),
        cost_estimate=LIGHT,
    )(zx, zx, taps, chan, bct, bcb, dtv, spread_matrix(width))


def mixer_backward(sg, zx, mixed, sin, coef, taps, chan, bct, bcb, dtv):
    rows = zx.shape[0]
    width2 = zx.shape[1] - 384
    width = width2 // 2
    side = width2 // 384
    chunks = rows // Q
    last = chunks - 1
    return pl.pallas_call(
        functools.partial(bwd_kernel, head_count=width // HEADDIM),
        grid=(chunks,),
        in_specs=[
            pl.BlockSpec((Q, width), lambda c: (last - c, 0)),
            pl.BlockSpec((Q, width2), lambda c: (last - c, 0)),
            pl.BlockSpec((16, width), lambda c: (jnp.maximum((last - c) * (Q // 16) - 1, 0), 1)),
            pl.BlockSpec((Q, width), lambda c: (last - c, 0)),
            pl.BlockSpec((1, LANES, width), lambda c: (last - c, 0, 0)),
            pl.BlockSpec((Q, 384), lambda c: (last - c, side)),
            pl.BlockSpec((8, 384), lambda c: (jnp.maximum((last - c) * (Q // 8) - 1, 0), side)),
            pl.BlockSpec((Q, LANES), lambda c: (last - c, 0)),
            whole((4, width)), whole((8, width)), whole((4, 256)), whole((1, 256)),
            whole((8, LANES)), whole((LANES, width)), whole((width, LANES)),
        ],
        out_specs=[
            pl.BlockSpec((Q, width2 + 384), lambda c: (last - c, 0)),
            whole((8, width)), whole((8, 256)), whole((8, LANES)),
        ],
        out_shape=[
            jax.ShapeDtypeStruct((rows, width2 + 384), bf16),
            jax.ShapeDtypeStruct((8, width), f32),
            jax.ShapeDtypeStruct((8, 256), f32),
            jax.ShapeDtypeStruct((8, LANES), f32),
        ],
        scratch_shapes=[
            pltpu.VMEM((Q + 8, width), f32),
            pltpu.VMEM((Q + 8, 256), f32),
            pltpu.VMEM((Q + 8, width), f32),
            pltpu.VMEM((Q + 8, 256), f32),
            pltpu.VMEM((LANES, width), f32),
            pltpu.VMEM((LANES, LANES), f32),
        ],
        compiler_params=pltpu.CompilerParams(
            dimension_semantics=("arbitrary",), vmem_limit_bytes=VMEM_LIMIT
        ),
        cost_estimate=LIGHT,
    )(sg, zx, zx, mixed, sin, zx, zx, coef, taps, chan, bct, bcb, dtv,
      spread_matrix(width), gather_matrix(width))


def pair_swap(v):
    return lax.ppermute(v, "tensor", ((0, 1), (1, 0)))


def both_rows(own, other, first):
    return jnp.where(
        first, jnp.concatenate([own, other], axis=0), jnp.concatenate([other, own], axis=0)
    )


def dp_factors():
    size = lax.axis_size("dp")
    known = {16: (2, 2, 4), 64: (2, 4, 2, 4)}
    return known.get(size, (size,))


def after(v, other):
    return lax.optimization_barrier((v, other))[0]


def row_blocks(v):
    size = lax.axis_size("dp")
    return v.reshape((size, v.shape[0] // size) + v.shape[1:])


def fold(blocks, level, start=None, finish=None, marks=()):
    factors = dp_factors()
    factor = factors[level]
    stride = 1
    for f in factors[:level]:
        stride *= f
    size = lax.axis_size("dp")
    place = (lax.axis_index("dp") // stride) % factor
    hops = []
    for i in range(size):
        here = (i // stride) % factor
        hops.append((i, i + ((here + 1) % factor - here) * stride))
    parts = blocks.reshape((blocks.shape[0] // factor, factor) + blocks.shape[1:])

    def pick(step):
        return lax.dynamic_index_in_dim(parts, (place + step) % factor, 1, keepdims=False)

    moving = pick(factor - 1)
    if start is not None:
        moving = after(moving, start)
    for step in range(factor - 1):
        if step < len(marks):
            moving = after(moving, marks[step])
        arrived = lax.ppermute(moving, "dp", hops)
        if finish is not None:
            arrived = after(arrived, finish)
        moving = (arrived.astype(f32) + pick(2 * factor - 2 - step).astype(f32)).astype(blocks.dtype)
    return moving, arrived


def head_lanes(v):
    return jnp.pad(v, ((0, LANES - v.shape[0]),))


def local(
    hidden,
    pre_gain,
    w_zx,
    w_bc,
    w_dt,
    conv_x,
    conv_x_bias,
    conv_bc,
    conv_bc_bias,
    dt_bias,
    a_log,
    d_skip,
    norm_gain,
    w_out,
    cotangent,
):
    layers = pre_gain.shape[0]
    own_count, depth = hidden.shape
    rows = own_count * lax.axis_size("tensor")
    width = w_zx.shape[-1]
    heads = dt_bias.shape[-1]
    tensor_index = lax.axis_index("tensor")
    first = tensor_index == 0

    def own_half(v):
        return lax.dynamic_slice_in_dim(v, tensor_index * own_count, own_count, 0)

    def other_half(v):
        return lax.dynamic_slice_in_dim(v, (1 - tensor_index) * own_count, own_count, 0)

    def gather_pair(v):
        return both_rows(v, pair_swap(v), first)

    in_weights = []
    out_weights = []
    for l in range(layers):
        shard = jnp.concatenate(
            [
                w_zx[l].reshape(w_zx.shape[1], -1),
                w_bc[l],
                jnp.pad(w_dt[l], ((0, 0), (0, LANES - heads))),
            ],
            axis=1,
        )
        in_weights.append(lax.all_gather(shard, "dp", axis=0, tiled=True))
        out_weights.append(lax.all_gather(w_out[l].T, "dp", axis=0, tiled=True))
    params = []
    for l in range(layers):
        chan = jnp.zeros((8, width), f32)
        chan = chan.at[0].set(conv_x_bias[l]).at[1].set(norm_gain[l])
        chan = chan.at[2].set(jnp.repeat(d_skip[l], HEADDIM))
        dtv = jnp.zeros((8, LANES), f32)
        dtv = dtv.at[0].set(head_lanes(dt_bias[l])).at[1].set(head_lanes(-jnp.exp(a_log[l])))
        params.append((conv_x[l], chan, conv_bc[l], conv_bc_bias[l][None, :], dtv))

    current = hidden.astype(f32)
    saved = []
    for l in range(layers):
        w_in = in_weights[l]
        rms = lax.rsqrt(jnp.mean(current * current, axis=1, keepdims=True) + epsilon)
        own_normed = (current * rms * pre_gain[l][None, :]).astype(bf16)
        if l == 0:
            arrived = pair_swap(jnp.concatenate([own_normed, cotangent], axis=0))
            normed = both_rows(own_normed, arrived[:own_count], first)
            cot = both_rows(cotangent, arrived[own_count:], first)
        else:
            normed = gather_pair(own_normed)
        zx = mm(normed, w_in)
        scaled, mixed, states, squares = mixer_forward(zx, *params[l])
        squares = jnp.sum(squares, axis=1).reshape(8, -1)
        squares = (squares + pair_swap(squares)).reshape(rows, 1)
        inv = lax.rsqrt(squares / INNER + epsilon)
        shaped = (scaled * inv).astype(bf16)
        other = mm_t(other_half(shaped), out_weights[l])
        own = mm_t(own_half(shaped), out_weights[l])
        outgoing = other.astype(bf16)
        if l == layers - 1:
            own_dot = jnp.sum(own_half(cot).astype(f32) * own, axis=1, keepdims=True)
            other_dot = jnp.sum(other_half(cot).astype(f32) * other, axis=1, keepdims=True)
            dots = jnp.where(
                first,
                jnp.concatenate([own_dot, other_dot], axis=0),
                jnp.concatenate([other_dot, own_dot], axis=0),
            ).reshape(8, -1)
            dots = dots + pair_swap(dots)
            last_dot = dots.reshape(rows, 1)
            arrived = pair_swap(after(outgoing, dots))
            last_own, last_arrived = own, arrived
        else:
            arrived = pair_swap(outgoing)
        lifted = own + arrived.astype(f32)
        saved.append((current, rms, normed, zx, shaped, mixed, states, inv, lifted))
        if l < layers - 1:
            current = current + lifted
    grad_rows = cotangent.astype(f32)
    outputs = [None] * layers
    out_parts = [None] * layers
    packed = [None] * layers
    for l in reversed(range(layers)):
        current, rms, normed, zx, shaped, mixed, states, inv, lifted = saved[l]
        w_in = in_weights[l]
        if l == layers - 1:
            out_grad = cot
            row_dot = last_dot
        else:
            own_grad = grad_rows.astype(bf16)
            out_grad = gather_pair(own_grad)
            own_dot = jnp.sum(own_grad.astype(f32) * lifted, axis=1).reshape(8, -1)
            row_dot = both_rows(own_dot.reshape(-1, 1), pair_swap(own_dot).reshape(-1, 1), first)
        coef = jnp.pad(
            jnp.concatenate([inv * inv * row_dot / INNER, inv], axis=1), ((0, 0), (0, LANES - 2))
        )
        shaped_grad = mm(out_grad, out_weights[l])
        grad_out = t_mm(out_grad, shaped).astype(bf16)
        low, gchan, gbc, gdt = mixer_backward(
            shaped_grad, zx, mixed, states, coef, *params[l]
        )
        if l == layers - 1:
            low, last_arrived = lax.optimization_barrier((low, last_arrived))
            hidden_out = saved[l][0] + last_own + last_arrived.astype(f32)
        if l == 0:
            low, done_in = lax.optimization_barrier((low, done_in))
        other = product_t(other_half(low), w_in, bf16)
        arrived = pair_swap(other)
        low = after(low, other)
        if l > 0:
            grad_in = t_product(normed, low, bf16, 0, 2 * width)
            done_in = lax.psum_scatter(grad_in, "dp", scatter_dimension=0, tiled=True)
            low = after(low, grad_in)
            own = product_t(own_half(low), w_in, f32)
            done_out = lax.psum_scatter(grad_out, "dp", scatter_dimension=0, tiled=True)
            arrived, own, done_out = lax.optimization_barrier((arrived, own, done_out))
            out_parts[l] = done_out
            low_last, normed_last = low, normed
        else:
            in_state = []
            for i in range(2):
                part = t_product(normed, low, bf16, i * width, width)
                in_state.append(fold(row_blocks(part), 0)[0])
                low = after(low, part)
            own = product_t(own_half(after(low, in_state[0])), w_in, f32)
            low = after(low, own)
        normed_grad = own + arrived.astype(f32)
        unit = current * rms
        weighted = normed_grad * pre_gain[l][None, :]
        grad_pre = jnp.sum(other.astype(f32) * other_half(normed).astype(f32), axis=0)
        grad_pre = grad_pre + jnp.sum(own * own_half(normed).astype(f32), axis=0)
        grad_pre = grad_pre / pre_gain[l]
        grad_rows = grad_rows + rms * (
            weighted - unit * jnp.mean(weighted * unit, axis=1, keepdims=True)
        )
        gchan = gchan.at[7].set(grad_pre)
        packed[l] = jnp.concatenate([gchan, gbc, gdt], axis=1)
        if l > 0:
            low_last = after(low_last, grad_rows)
            side_last = t_mm(normed_last, low_last[:, 2 * width : 2 * width + 256 + heads])
        else:
            side = t_mm(normed, low[:, 2 * width : 2 * width + 256 + heads])
    done_out = lax.psum_scatter(grad_out, "dp", scatter_dimension=0, tiled=True)
    done_out = after(done_out, (own, in_state[1]))
    small = jnp.stack(packed)
    spare = small.reshape(depth, -1)
    side_width = 256 + heads
    side = jnp.concatenate([side, side_last, spare], axis=1)
    side = jnp.pad(side, ((0, 0), (0, -side.shape[1] % LANES)))
    side = after(side, done_out)
    side_own = lax.psum_scatter(side, "dp", scatter_dimension=0, tiled=True)
    shares = side_own[:, 2 * side_width : 2 * side_width + spare.shape[1]].reshape(-1)
    shares = lax.all_gather(shares, ("dp", "tensor"), axis=0, tiled=False)
    shares = shares.reshape(-1, lax.axis_size("tensor"), shares.shape[-1])
    mine = lax.dynamic_index_in_dim(shares, tensor_index, 1, keepdims=False).reshape(small.shape)
    both = jnp.sum(shares, axis=1).reshape(small.shape)
    row = lax.broadcasted_iota(jnp.int32, small.shape, 1)
    col = lax.broadcasted_iota(jnp.int32, small.shape, 2)
    shared = ((row == 7) & (col < width)) | ((col >= width) & (col < width + 256))
    small = jnp.where(shared, both, mine)
    queue = in_state
    for level in range(1, len(dp_factors())):
        last_level = level == len(dp_factors()) - 1
        last_arrival = None
        for n in range(len(queue)):
            queue[n], last_arrival = fold(
                queue[n], level, start=None if last_level else last_arrival
            )
    done = [q.reshape(q.shape[1:]) for q in queue]
    out_parts[0] = done_out
    in_parts = [jnp.concatenate(done, axis=1), done_in]
    side_parts = [side_own[:, :side_width], side_own[:, side_width : 2 * side_width]]
    for l in range(layers):
        grad_bc = side_parts[l][:, :256]
        outputs[l] = (
            in_parts[l].astype(f32).reshape(-1, 2, width),
            grad_bc + pair_swap(grad_bc),
            side_parts[l][:, 256:],
            out_parts[l].astype(f32).T,
        )
    grad_w_zx, grad_w_bc, grad_w_dt, grad_w_out = (
        jnp.stack([o[i] for o in outputs]) for i in range(4)
    )
    return (
        hidden_out,
        grad_rows,
        small[:, 7, :width],
        grad_w_zx,
        grad_w_bc,
        grad_w_dt,
        small[:, 0:4, :width],
        small[:, 4, :width],
        small[:, 0:4, width : width + 256],
        small[:, 4, width : width + 256],
        small[:, 0, width + 256 : width + 256 + heads],
        small[:, 1, width + 256 : width + 256 + heads],
        jnp.sum(small[:, 6, :width].reshape(layers, heads, HEADDIM), axis=2),
        small[:, 5, :width],
        grad_w_out,
    )


def solution(mesh):
    return jax.shard_map(
        local,
        mesh=mesh,
        in_specs=(
            P(("dp", "tensor"), None),
            P(),
            P(None, "dp", None, "tensor"),
            P(None, "dp", None),
            P(None, "dp", "tensor"),
            P(None, None, "tensor"),
            P(None, "tensor"),
            P(),
            P(),
            P(None, "tensor"),
            P(None, "tensor"),
            P(None, "tensor"),
            P(None, "tensor"),
            P(None, "tensor", "dp"),
            P(("dp", "tensor"), None),
        ),
        out_specs=(
            P(("dp", "tensor"), None),
            P(("dp", "tensor"), None),
            P(),
            P(None, "dp", None, "tensor"),
            P(None, "dp", None),
            P(None, "dp", "tensor"),
            P(None, None, "tensor"),
            P(None, "tensor"),
            P(),
            P(),
            P(None, "tensor"),
            P(None, "tensor"),
            P(None, "tensor"),
            P(None, "tensor"),
            P(None, "tensor", "dp"),
        ),
        check_vma=False,
    )
```

```python
import functools
import jax
import jax.numpy as jnp
from jax import lax
from jax.experimental import pallas as pl
from jax.experimental.pallas import tpu as pltpu
from jax.sharding import PartitionSpec as P

HEADDIM = 64
INNER = 3072
LANES = 128
Q = 128
GROUP = 256
LOG2E = 1.4426950408889634
epsilon = 1e-05
highest = lax.Precision.HIGHEST
bf16 = jnp.bfloat16
f32 = jnp.float32


def sigmoid(v):
    return 0.5 * jnp.tanh(0.5 * v) + 0.5


def mm(a, b, precision=None):
    return lax.dot_general(
        a, b, (((1,), (0,)), ((), ())), precision=precision, preferred_element_type=f32
    )


def mm_t(a, b):
    return lax.dot_general(a, b, (((1,), (1,)), ((), ())), preferred_element_type=f32)


def t_mm(a, b):
    return lax.dot_general(a, b, (((0,), (0,)), ((), ())), preferred_element_type=f32)


def iota2(shape, dim):
    return lax.broadcasted_iota(jnp.int32, shape, dim)


def split_lanes(v):
    high = v.astype(bf16).astype(f32)
    rest = v - high
    return (high + pltpu.roll(rest, 32, axis=1)).astype(bf16)


def taps_sum(ext_ref, taps_ref, bias_ref, columns):
    total = bias_ref[0:1, columns]
    for k in range(4):
        total = total + taps_ref[k : k + 1, columns] * ext_ref[5 + k : 5 + k + Q, columns]
    return total


def chunk_terms(bcdt_ref, bext_ref, bct_ref, bcb_ref, dtv_ref, head_count):
    bext_ref[8 : 8 + Q, :] = bcdt_ref[:, 0:256]
    z = taps_sum(bext_ref, bct_ref, bcb_ref, slice(0, 256))
    s = sigmoid(z)
    bc = z * s
    dsilu = s * (1.0 + z * (1.0 - s))
    b_part = bc[:, 0:128]
    c_part = bc[:, 128:256]
    pre = bcdt_ref[:, 256:384] + dtv_ref[0:1, :]
    live = iota2((Q, LANES), 1) < head_count
    step = jnp.where(live, jnp.maximum(pre, 0.0) + jnp.log1p(jnp.exp(-jnp.abs(pre))), 0.0)
    decay = step * dtv_ref[1:2, :]
    rows = iota2((Q, Q), 0)
    cols = iota2((Q, Q), 1)
    lower = rows >= cols
    cum = mm(lower.astype(f32), decay, highest)
    return b_part, c_part, dsilu, pre, live, step, decay, cum, lower


def fwd_kernel(
    zx_ref, bcdt_ref, taps_ref, chan_ref, bct_ref, bcb_ref, dtv_ref, spread_ref,
    sh_ref, mixed_ref, sin_ref, ssq_ref, ext_ref, bext_ref, state_ref, *, head_count,
):
    width = sh_ref.shape[1]

    @pl.when(pl.program_id(0) == 0)
    def _():
        ext_ref[0:8, :] = jnp.zeros((8, width), f32)
        bext_ref[0:8, :] = jnp.zeros((8, 256), f32)
        state_ref[...] = jnp.zeros_like(state_ref)

    @pl.when(pl.program_id(0) > 0)
    def _():
        ext_ref[0:8, :] = ext_ref[Q : Q + 8, :]
        bext_ref[0:8, :] = bext_ref[Q : Q + 8, :]

    b_part, c_part, _, _, live, step, decay, cum, lower = chunk_terms(
        bcdt_ref, bext_ref, bct_ref, bcb_ref, dtv_ref, head_count
    )
    cum2 = cum * LOG2E
    across = cum2.T
    last = cum2[Q - 1 : Q, :]
    bb = b_part.astype(bf16)
    cb = c_part.astype(bf16)
    bt = b_part.T.astype(bf16)
    c_both = jnp.concatenate([cb, (c_part - cb.astype(f32)).astype(bf16)], axis=1)
    scores = jnp.where(lower, mm(c_part, b_part.T, highest), 0.0)
    step_l = split_lanes(step)
    grow_l = split_lanes(jnp.where(live, jnp.exp2(cum2), 0.0))
    left_l = split_lanes(jnp.where(live, jnp.exp2(last - cum2), 0.0))
    all_l = split_lanes(jnp.where(live[0:8], jnp.exp2(jnp.broadcast_to(last, (8, LANES))), 0.0))
    half = iota2((Q, LANES), 1) < HEADDIM
    ssq = jnp.zeros((Q, LANES), f32)
    for g in range(width // GROUP):
        columns = slice(g * GROUP, (g + 1) * GROUP)
        spread = spread_ref[:, columns]
        step_e = mm(step_l, spread)
        grow_e = mm(grow_l, spread)
        left_e = mm(left_l, spread)
        all_e = mm(all_l, spread)[0:1, :]
        ext_ref[8 : 8 + Q, columns] = zx_ref[:, width + g * GROUP : width + (g + 1) * GROUP].astype(f32)
        z = taps_sum(ext_ref, taps_ref, chan_ref, columns)
        xc = z * sigmoid(z)
        v = xc * step_e
        vb = v.astype(bf16)
        vl = (v - vb.astype(f32)).astype(bf16)
        state = state_ref[:, columns]
        state_b = state.astype(bf16)
        sin_ref[0, :, columns] = state_b
        state_l = (state - state_b.astype(f32)).astype(bf16)
        y = mm(c_both, jnp.concatenate([state_b, state_b], axis=0)) + mm(cb, state_l)
        y = y * grow_e
        parts = []
        for pair in range(GROUP // LANES):
            head = (g * GROUP + pair * LANES) // HEADDIM
            lanes = slice(pair * LANES, (pair + 1) * LANES)
            vp, vq = vb[:, lanes], vl[:, lanes]
            highs, lows = [], []
            for h in (head, head + 1):
                d = cum2[:, h : h + 1] - across[h : h + 1, :]
                m = scores * jnp.exp2(-jnp.abs(d))
                mb = m.astype(bf16)
                highs.append(mb)
                lows.append((m - mb.astype(f32)).astype(bf16))
            block = [jnp.where(half, vp, 0), jnp.where(half, 0, vp)]
            block_l = [jnp.where(half, vq, 0), jnp.where(half, 0, vq)]
            parts.append(
                mm(
                    jnp.concatenate(highs + lows + highs, axis=1),
                    jnp.concatenate(block + block + block_l, axis=0),
                )
            )
        y = y + jnp.concatenate(parts, axis=1)
        state_ref[:, columns] = state * all_e + mm(bt, (v * left_e).astype(bf16))
        mixed = y + chan_ref[2:3, columns] * xc
        mixed_ref[:, columns] = mixed.astype(bf16)
        gate = zx_ref[:, columns].astype(f32)
        gated = mixed * (gate * sigmoid(gate))
        squares = gated * gated
        ssq = ssq + squares[:, 0:LANES] + squares[:, LANES : 2 * LANES]
        sh_ref[:, columns] = gated * chan_ref[1:2, columns]
    ssq_ref[...] = ssq


def bwd_kernel(
    sg_ref, zx_ref, xprev_ref, mixed_ref, sin_ref, bcdt_ref, bcprev_ref, coef_ref,
    taps_ref, chan_ref, bct_ref, bcb_ref, dtv_ref, spread_ref, gather_ref,
    low_ref, gchan_ref, gbc_ref, gdt_ref,
    ext_ref, bext_ref, dz_ref, dbz_ref, dstate_ref, colsum_ref, *, head_count,
):
    width = sg_ref.shape[1]
    step_id = pl.program_id(0)
    is_first = step_id == pl.num_programs(0) - 1

    @pl.when(step_id == 0)
    def _():
        dz_ref[Q : Q + 8, :] = jnp.zeros((8, width), f32)
        dbz_ref[Q : Q + 8, :] = jnp.zeros((8, 256), f32)
        dstate_ref[...] = jnp.zeros_like(dstate_ref)
        gchan_ref[...] = jnp.zeros_like(gchan_ref)
        gbc_ref[...] = jnp.zeros_like(gbc_ref)
        gdt_ref[...] = jnp.zeros_like(gdt_ref)
        colsum_ref[...] = jnp.zeros_like(colsum_ref)

    @pl.when(step_id > 0)
    def _():
        dz_ref[Q : Q + 8, :] = dz_ref[0:8, :]
        dbz_ref[Q : Q + 8, :] = dbz_ref[0:8, :]

    keep = jnp.where(is_first, 0.0, 1.0)
    ext_ref[0:8, :] = xprev_ref[8:16, :].astype(f32) * keep
    bext_ref[0:8, :] = bcprev_ref[:, 0:256] * keep
    b_part, c_part, bc_dsilu, dt_pre, live, step, decay, cum, lower = chunk_terms(
        bcdt_ref, bext_ref, bct_ref, bcb_ref, dtv_ref, head_count
    )
    cum2 = cum * LOG2E
    across = cum2.T
    last = cum2[Q - 1 : Q, :]
    bb = b_part.astype(bf16)
    cb = c_part.astype(bf16)
    bt = b_part.T.astype(bf16)
    ct = c_part.T.astype(bf16)
    upper = iota2((Q, Q), 0) <= iota2((Q, Q), 1)
    scores = jnp.where(lower, mm(c_part, b_part.T, highest), 0.0)
    scores_t = scores.T
    step_l = split_lanes(step)
    grow_l = split_lanes(jnp.where(live, jnp.exp2(cum2), 0.0))
    left_l = split_lanes(jnp.where(live, jnp.exp2(last - cum2), 0.0))
    all_l = split_lanes(jnp.where(live[0:8], jnp.exp2(jnp.broadcast_to(last, (8, LANES))), 0.0))
    half = iota2((Q, LANES), 1) < HEADDIM
    coef = coef_ref[:, 0:1]
    inv = coef_ref[:, 1:2]
    d_scores = jnp.zeros((Q, Q), f32)
    d_c = jnp.zeros((Q, LANES), f32)
    d_b = jnp.zeros((Q, LANES), f32)
    row_sums = jnp.zeros((Q, LANES), f32)
    red_step = jnp.zeros((Q, LANES), f32)
    red_in = jnp.zeros((Q, LANES), f32)
    red_out = jnp.zeros((Q, LANES), f32)
    red_all = jnp.zeros((8, LANES), f32)
    ones = jnp.ones((16, Q), bf16)
    pair_rows = iota2((2 * Q, LANES), 0) // Q
    pair_cols = iota2((2 * Q, LANES), 1)
    for g in range(width // GROUP):
        columns = slice(g * GROUP, (g + 1) * GROUP)
        spread = spread_ref[:, columns]
        gather = gather_ref[columns, :]
        step_e = mm(step_l, spread)
        grow_e = mm(grow_l, spread)
        left_e = mm(left_l, spread)
        all_e = mm(all_l, spread)[0:1, :]
        ext_ref[8 : 8 + Q, columns] = zx_ref[:, width + g * GROUP : width + (g + 1) * GROUP].astype(f32)
        z = taps_sum(ext_ref, taps_ref, chan_ref, columns)
        s = sigmoid(z)
        xc = z * s
        x_dsilu = s * (1.0 + z * (1.0 - s))
        gate = zx_ref[:, columns].astype(f32)
        gs = sigmoid(gate)
        act = gate * gs
        act_d = gs * (1.0 + gate * (1.0 - gs))
        mixed = mixed_ref[:, columns].astype(f32)
        gated = mixed * act
        sg = sg_ref[:, columns] * inv
        grad_gated = sg * chan_ref[1:2, columns] - gated * coef
        dy = grad_gated * act
        low_ref[:, columns] = (grad_gated * mixed * act_d).astype(bf16)
        gchan_ref[5:6, columns] += jnp.sum(sg * gated, axis=0, keepdims=True)
        gchan_ref[6:7, columns] += jnp.sum(dy * xc, axis=0, keepdims=True)
        dyb = dy.astype(bf16)
        v = xc * step_e
        vb = v.astype(bf16)
        sin = sin_ref[0, :, columns]
        ey = dy * grow_e
        eyb = ey.astype(bf16)
        inter = ey * mm(cb, sin)
        dstate = dstate_ref[:, columns]
        dstate_b = dstate.astype(bf16)
        dv_state = mm(bb, dstate_b) * left_e
        d_c = d_c + mm_t(eyb, sin)
        d_b = d_b + mm_t((v * left_e).astype(bf16), dstate_b)
        kept = jnp.sum(sin.astype(f32) * dstate, axis=0, keepdims=True) * all_e
        dstate_ref[:, columns] = dstate * all_e + mm(ct, eyb)
        parts = []
        for pair in range(GROUP // LANES):
            lanes = slice(pair * LANES, (pair + 1) * LANES)
            head = (g * GROUP + pair * LANES) // HEADDIM
            vp = vb[:, lanes]
            dp = dyb[:, lanes]
            v_block = jnp.concatenate([jnp.where(half, vp, 0), jnp.where(half, 0, vp)], axis=0)
            d_block = jnp.concatenate([jnp.where(half, dp, 0), jnp.where(half, 0, dp)], axis=0)
            dm = mm_t(dp, v_block)
            mts = []
            ws = []
            for i, h in enumerate((head, head + 1)):
                d = cum2[:, h : h + 1] - across[h : h + 1, :]
                e = jnp.exp2(-jnp.abs(d))
                dme = dm[:, i * Q : (i + 1) * Q] * e
                d_scores = d_scores + dme
                mts.append((scores_t * e).astype(bf16))
                ws.append((dme * scores).astype(bf16))
            parts.append(mm(jnp.concatenate(mts, axis=1), d_block))
            w = jnp.concatenate(ws, axis=1)
            picks = (pair_cols == head + pair_rows).astype(bf16)
            row_sums = row_sums + mm(w, picks)
            sums = mm(ones, w)
            colsum_ref[head : head + 1, :] = sums[0:1, 0:Q]
            colsum_ref[head + 1 : head + 2, :] = sums[0:1, Q : 2 * Q]
        dv = jnp.concatenate(parts, axis=1) + dv_state
        red_step = red_step + mm((dv * xc).astype(bf16), gather)
        red_in = red_in + mm(inter.astype(bf16), gather)
        red_out = red_out + mm((v * dv_state).astype(bf16), gather)
        red_all = red_all + mm(jnp.broadcast_to(kept, (8, GROUP)), gather.astype(f32), highest)
        dz = (dv * step_e + chan_ref[2:3, columns] * dy) * x_dsilu
        dz_ref[0:Q, columns] = dz
        dx = jnp.zeros((Q, GROUP), f32)
        for k in range(4):
            dx = dx + taps_ref[k : k + 1, columns] * dz_ref[3 - k : 3 - k + Q, columns]
            gchan_ref[k : k + 1, columns] += jnp.sum(
                dz * ext_ref[5 + k : 5 + k + Q, columns], axis=0, keepdims=True
            )
        gchan_ref[4:5, columns] += jnp.sum(dz, axis=0, keepdims=True)
        low_ref[:, width + g * GROUP : width + (g + 1) * GROUP] = dx.astype(bf16)
    through = row_sums - colsum_ref[...].T + red_in
    d_decay = mm(upper.astype(f32), through, highest) + mm(
        jnp.where(upper, 0.0, 1.0), red_out, highest
    ) + red_all[0:1, :]
    d_decay = jnp.where(live, d_decay, 0.0)
    d_pre = (red_step + d_decay * dtv_ref[1:2, :]) * sigmoid(dt_pre)
    d_pre = jnp.where(live, d_pre, 0.0)
    gdt_ref[0:1, :] += jnp.sum(d_pre, axis=0, keepdims=True)
    gdt_ref[1:2, :] += jnp.sum(d_decay * decay, axis=0, keepdims=True)
    low_ref[:, 2 * width + 256 : 2 * width + 384] = d_pre.astype(bf16)
    d_scores = jnp.where(lower, d_scores, 0.0)
    d_c = d_c + mm(d_scores, b_part, highest)
    d_b = d_b + mm(d_scores.T, c_part, highest)
    dbz = jnp.concatenate([d_b, d_c], axis=1) * bc_dsilu
    dbz_ref[0:Q, :] = dbz
    dbc = jnp.zeros((Q, 256), f32)
    for k in range(4):
        dbc = dbc + bct_ref[k : k + 1, :] * dbz_ref[3 - k : 3 - k + Q, :]
        gbc_ref[k : k + 1, :] += jnp.sum(
            dbz * bext_ref[5 + k : 5 + k + Q, :], axis=0, keepdims=True
        )
    gbc_ref[4:5, :] += jnp.sum(dbz, axis=0, keepdims=True)
    low_ref[:, 2 * width : 2 * width + 256] = dbc.astype(bf16)


def spread_matrix(width):
    heads = jnp.arange(width) // HEADDIM
    lanes = jnp.arange(LANES)
    return ((lanes[:, None] == heads[None, :]) | (lanes[:, None] == heads[None, :] + 32)).astype(bf16)


def gather_matrix(width):
    heads = jnp.arange(width) // HEADDIM
    return (heads[:, None] == jnp.arange(LANES)[None, :]).astype(bf16)


def whole(shape):
    return pl.BlockSpec(shape, lambda c: (0,) * len(shape))


VMEM_LIMIT = 48 * 1024 * 1024
LIGHT = pl.CostEstimate(flops=1000, bytes_accessed=1000, transcendentals=0)


def product_t(a, b, out_dtype, half, columns=512):
    rows = a.shape[0] // 2
    count, depth = b.shape

    def body(half_ref, a_ref, b_ref, o_ref):
        o_ref[...] = mm_t(a_ref[...], b_ref[...]).astype(out_dtype)

    return pl.pallas_call(
        body,
        grid_spec=pltpu.PrefetchScalarGridSpec(
            num_scalar_prefetch=1,
            grid=(count // columns,),
            in_specs=[
                pl.BlockSpec((rows, depth), lambda j, h: (h[0], 0)),
                pl.BlockSpec((columns, depth), lambda j, h: (j, 0)),
            ],
            out_specs=pl.BlockSpec((rows, columns), lambda j, h: (0, j)),
        ),
        out_shape=jax.ShapeDtypeStruct((rows, count), out_dtype),
        compiler_params=pltpu.CompilerParams(vmem_limit_bytes=VMEM_LIMIT),
        cost_estimate=LIGHT,
    )(half.reshape(1), a, b)


def t_product(a, b, out_dtype, first, count, columns=512):
    depth, rows = a.shape
    offset = first // columns

    def body(a_ref, b_ref, o_ref):
        o_ref[...] = t_mm(a_ref[...], b_ref[...]).astype(out_dtype)

    return pl.pallas_call(
        body,
        grid=(count // columns,),
        in_specs=[
            pl.BlockSpec((depth, rows), lambda j: (0, 0)),
            pl.BlockSpec((depth, columns), lambda j: (0, offset + j)),
        ],
        out_specs=pl.BlockSpec((rows, columns), lambda j: (0, j)),
        out_shape=jax.ShapeDtypeStruct((rows, count), out_dtype),
        compiler_params=pltpu.CompilerParams(vmem_limit_bytes=VMEM_LIMIT),
        cost_estimate=LIGHT,
    )(a, b)


def mixer_forward(zx, taps, chan, bct, bcb, dtv):
    rows = zx.shape[0]
    width2 = zx.shape[1] - 384
    width = width2 // 2
    side = width2 // 384
    chunks = rows // Q
    return pl.pallas_call(
        functools.partial(fwd_kernel, head_count=width // HEADDIM),
        grid=(chunks,),
        in_specs=[
            pl.BlockSpec((Q, width2), lambda c: (c, 0)),
            pl.BlockSpec((Q, 384), lambda c: (c, side)),
            whole((4, width)), whole((8, width)), whole((4, 256)), whole((1, 256)),
            whole((8, LANES)), whole((LANES, width)),
        ],
        out_specs=[
            pl.BlockSpec((Q, width), lambda c: (c, 0)),
            pl.BlockSpec((Q, width), lambda c: (c, 0)),
            pl.BlockSpec((1, LANES, width), lambda c: (c, 0, 0)),
            pl.BlockSpec((Q, LANES), lambda c: (c, 0)),
        ],
        out_shape=[
            jax.ShapeDtypeStruct((rows, width), f32),
            jax.ShapeDtypeStruct((rows, width), bf16),
            jax.ShapeDtypeStruct((chunks, LANES, width), bf16),
            jax.ShapeDtypeStruct((rows, LANES), f32),
        ],
        scratch_shapes=[
            pltpu.VMEM((Q + 8, width), f32),
            pltpu.VMEM((Q + 8, 256), f32),
            pltpu.VMEM((LANES, width), f32),
        ],
        compiler_params=pltpu.CompilerParams(
            dimension_semantics=("arbitrary",), vmem_limit_bytes=VMEM_LIMIT
        ),
        cost_estimate=LIGHT,
    )(zx, zx, taps, chan, bct, bcb, dtv, spread_matrix(width))


def mixer_backward(sg, zx, mixed, sin, coef, taps, chan, bct, bcb, dtv):
    rows = zx.shape[0]
    width2 = zx.shape[1] - 384
    width = width2 // 2
    side = width2 // 384
    chunks = rows // Q
    last = chunks - 1
    return pl.pallas_call(
        functools.partial(bwd_kernel, head_count=width // HEADDIM),
        grid=(chunks,),
        in_specs=[
            pl.BlockSpec((Q, width), lambda c: (last - c, 0)),
            pl.BlockSpec((Q, width2), lambda c: (last - c, 0)),
            pl.BlockSpec((16, width), lambda c: (jnp.maximum((last - c) * (Q // 16) - 1, 0), 1)),
            pl.BlockSpec((Q, width), lambda c: (last - c, 0)),
            pl.BlockSpec((1, LANES, width), lambda c: (last - c, 0, 0)),
            pl.BlockSpec((Q, 384), lambda c: (last - c, side)),
            pl.BlockSpec((8, 384), lambda c: (jnp.maximum((last - c) * (Q // 8) - 1, 0), side)),
            pl.BlockSpec((Q, LANES), lambda c: (last - c, 0)),
            whole((4, width)), whole((8, width)), whole((4, 256)), whole((1, 256)),
            whole((8, LANES)), whole((LANES, width)), whole((width, LANES)),
        ],
        out_specs=[
            pl.BlockSpec((Q, width2 + 384), lambda c: (last - c, 0)),
            whole((8, width)), whole((8, 256)), whole((8, LANES)),
        ],
        out_shape=[
            jax.ShapeDtypeStruct((rows, width2 + 384), bf16),
            jax.ShapeDtypeStruct((8, width), f32),
            jax.ShapeDtypeStruct((8, 256), f32),
            jax.ShapeDtypeStruct((8, LANES), f32),
        ],
        scratch_shapes=[
            pltpu.VMEM((Q + 8, width), f32),
            pltpu.VMEM((Q + 8, 256), f32),
            pltpu.VMEM((Q + 8, width), f32),
            pltpu.VMEM((Q + 8, 256), f32),
            pltpu.VMEM((LANES, width), f32),
            pltpu.VMEM((LANES, LANES), f32),
        ],
        compiler_params=pltpu.CompilerParams(
            dimension_semantics=("arbitrary",), vmem_limit_bytes=VMEM_LIMIT
        ),
        cost_estimate=LIGHT,
    )(sg, zx, zx, mixed, sin, zx, zx, coef, taps, chan, bct, bcb, dtv,
      spread_matrix(width), gather_matrix(width))


def pair_swap(v):
    return lax.ppermute(v, "tensor", ((0, 1), (1, 0)))


def both_rows(own, other, first):
    return jnp.where(
        first, jnp.concatenate([own, other], axis=0), jnp.concatenate([other, own], axis=0)
    )


def dp_factors():
    size = lax.axis_size("dp")
    known = {16: (2, 2, 4), 64: (2, 4, 2, 4)}
    return known.get(size, (size,))


def after(v, other):
    return lax.optimization_barrier((v, other))[0]


def row_blocks(v):
    size = lax.axis_size("dp")
    return v.reshape((size, v.shape[0] // size) + v.shape[1:])


def fold(blocks, level, start=None, finish=None, marks=()):
    factors = dp_factors()
    factor = factors[level]
    stride = 1
    for f in factors[:level]:
        stride *= f
    size = lax.axis_size("dp")
    place = (lax.axis_index("dp") // stride) % factor
    hops = []
    for i in range(size):
        here = (i // stride) % factor
        hops.append((i, i + ((here + 1) % factor - here) * stride))
    parts = blocks.reshape((blocks.shape[0] // factor, factor) + blocks.shape[1:])

    def pick(step):
        return lax.dynamic_index_in_dim(parts, (place + step) % factor, 1, keepdims=False)

    moving = pick(factor - 1)
    if start is not None:
        moving = after(moving, start)
    for step in range(factor - 1):
        if step < len(marks):
            moving = after(moving, marks[step])
        arrived = lax.ppermute(moving, "dp", hops)
        if finish is not None:
            arrived = after(arrived, finish)
        moving = (arrived.astype(f32) + pick(2 * factor - 2 - step).astype(f32)).astype(blocks.dtype)
    return moving, arrived


def sum_devices(v, spans):
    size = lax.axis_size("dp")
    for span in spans:
        v = v + lax.ppermute(v, "dp", [(i, i ^ span) for i in range(size)])
    return v


def ring_gather(shard):
    size = lax.axis_size("dp")
    chips = size // 2
    order = {8: (0, 2, 4, 6, 7, 5, 3, 1)}.get(chips, tuple(range(chips)))
    index = lax.axis_index("dp")
    core = index % 2
    place = jnp.asarray([order.index(c) for c in range(chips)], jnp.int32)[index // 2]
    chip_at = jnp.asarray(order, jnp.int32)
    onward, back = [], []
    for k in range(chips):
        here, there = order[k], order[(k + 1) % chips]
        for c in range(2):
            onward.append((here * 2 + c, there * 2 + c))
            back.append((there * 2 + c, here * 2 + c))
    cores = [(i, i ^ 1) for i in range(size)]
    whole_array = jnp.zeros((size,) + shard.shape, shard.dtype)
    half = chips // 2
    cut = (shard.shape[1] // 256) * LANES

    def swap(piece):
        return lax.ppermute(piece, "dp", cores)

    def put(target, piece, other, position):
        chip = chip_at[position % chips]
        target = lax.dynamic_update_slice(target, piece[None], (chip * 2 + core, 0, 0))
        return lax.dynamic_update_slice(target, other[None], (chip * 2 + 1 - core, 0, 0))

    ahead = behind = shard
    others = [swap(shard)]
    places = [(shard, place)]
    for step in range(1, half):
        ahead = lax.ppermute(ahead, "dp", onward)
        behind = lax.ppermute(behind, "dp", back)
        ahead, behind, others = lax.optimization_barrier((ahead, behind, others))
        places += [(ahead, place - step + chips), (behind, place + step)]
        others = others + [swap(ahead), swap(behind)]
    reached = behind
    piece = jnp.concatenate(
        [
            lax.ppermute(ahead[:, :cut], "dp", onward),
            lax.ppermute(behind[:, cut:], "dp", back),
        ],
        axis=1,
    )
    piece, others = lax.optimization_barrier((piece, others))
    places.append((piece, place + half))
    others = others + [swap(piece)]
    for (got, position), other in zip(places, others):
        whole_array = put(whole_array, got, other, position)
    return whole_array.reshape((-1,) + shard.shape[1:]), reached


def head_lanes(v):
    return jnp.pad(v, ((0, LANES - v.shape[0]),))


def local(
    hidden,
    pre_gain,
    w_zx,
    w_bc,
    w_dt,
    conv_x,
    conv_x_bias,
    conv_bc,
    conv_bc_bias,
    dt_bias,
    a_log,
    d_skip,
    norm_gain,
    w_out,
    cotangent,
):
    layers = pre_gain.shape[0]
    own_count, depth = hidden.shape
    rows = own_count * lax.axis_size("tensor")
    width = w_zx.shape[-1]
    heads = dt_bias.shape[-1]
    tensor_index = lax.axis_index("tensor")
    first = tensor_index == 0

    def own_half(v):
        return lax.dynamic_slice_in_dim(v, tensor_index * own_count, own_count, 0)

    def other_half(v):
        return lax.dynamic_slice_in_dim(v, (1 - tensor_index) * own_count, own_count, 0)

    def gather_pair(v):
        return both_rows(v, pair_swap(v), first)

    in_weights = []
    out_weights = []
    for l in range(layers):
        shard = jnp.concatenate(
            [
                w_zx[l].reshape(w_zx.shape[1], -1),
                w_bc[l],
                jnp.pad(w_dt[l], ((0, 0), (0, LANES - heads))),
            ],
            axis=1,
        )
        out_shard = w_out[l].T
        if l == 0:
            gathered, reached = ring_gather(shard)
            in_weights.append(gathered)
            out_shard = after(out_shard, reached)
        else:
            shard = after(shard, reached)
            in_weights.append(lax.all_gather(shard, "dp", axis=0, tiled=True))
        out_weights.append(lax.all_gather(out_shard, "dp", axis=0, tiled=True))
    params = []
    for l in range(layers):
        chan = jnp.zeros((8, width), f32)
        chan = chan.at[0].set(conv_x_bias[l]).at[1].set(norm_gain[l])
        chan = chan.at[2].set(jnp.repeat(d_skip[l], HEADDIM))
        dtv = jnp.zeros((8, LANES), f32)
        dtv = dtv.at[0].set(head_lanes(dt_bias[l])).at[1].set(head_lanes(-jnp.exp(a_log[l])))
        params.append((conv_x[l], chan, conv_bc[l], conv_bc_bias[l][None, :], dtv))

    current = hidden.astype(f32)
    saved = []
    for l in range(layers):
        w_in = in_weights[l]
        rms = lax.rsqrt(jnp.mean(current * current, axis=1, keepdims=True) + epsilon)
        own_normed = (current * rms * pre_gain[l][None, :]).astype(bf16)
        if l == 0:
            arrived = pair_swap(jnp.concatenate([own_normed, cotangent], axis=0))
            normed = both_rows(own_normed, arrived[:own_count], first)
            cot = both_rows(cotangent, arrived[own_count:], first)
        else:
            normed = gather_pair(own_normed)
        zx = mm(normed, w_in)
        scaled, mixed, states, squares = mixer_forward(zx, *params[l])
        squares = jnp.sum(squares, axis=1).reshape(8, -1)
        squares = (squares + pair_swap(squares)).reshape(rows, 1)
        inv = lax.rsqrt(squares / INNER + epsilon)
        shaped = (scaled * inv).astype(bf16)
        other = mm_t(other_half(shaped), out_weights[l])
        own = mm_t(own_half(shaped), out_weights[l])
        outgoing = other.astype(bf16)
        if l == layers - 1:
            own_dot = jnp.sum(own_half(cot).astype(f32) * own, axis=1, keepdims=True)
            other_dot = jnp.sum(other_half(cot).astype(f32) * other, axis=1, keepdims=True)
            dots = jnp.where(
                first,
                jnp.concatenate([own_dot, other_dot], axis=0),
                jnp.concatenate([other_dot, own_dot], axis=0),
            ).reshape(8, -1)
            dots = dots + pair_swap(dots)
            last_dot = dots.reshape(rows, 1)
            arrived = pair_swap(after(outgoing, dots))
            last_own, last_arrived = own, arrived
        else:
            arrived = pair_swap(outgoing)
        lifted = own + arrived.astype(f32)
        saved.append((current, rms, normed, zx, shaped, mixed, states, inv, lifted))
        if l < layers - 1:
            current = current + lifted
    grad_rows = cotangent.astype(f32)
    outputs = [None] * layers
    out_parts = [None] * layers
    packed = [None] * layers
    for l in reversed(range(layers)):
        current, rms, normed, zx, shaped, mixed, states, inv, lifted = saved[l]
        w_in = in_weights[l]
        if l == layers - 1:
            out_grad = cot
            row_dot = last_dot
        else:
            own_grad = grad_rows.astype(bf16)
            out_grad = gather_pair(own_grad)
            own_dot = jnp.sum(own_grad.astype(f32) * lifted, axis=1).reshape(8, -1)
            row_dot = both_rows(own_dot.reshape(-1, 1), pair_swap(own_dot).reshape(-1, 1), first)
        coef = jnp.pad(
            jnp.concatenate([inv * inv * row_dot / INNER, inv], axis=1), ((0, 0), (0, LANES - 2))
        )
        shaped_grad = mm(out_grad, out_weights[l])
        grad_out = t_mm(out_grad, shaped).astype(bf16)
        low, gchan, gbc, gdt = mixer_backward(
            shaped_grad, zx, mixed, states, coef, *params[l]
        )
        if l == layers - 1:
            low, last_arrived = lax.optimization_barrier((low, last_arrived))
            hidden_out = saved[l][0] + last_own + last_arrived.astype(f32)
        if l == 0:
            low, done_in = lax.optimization_barrier((low, done_in))
        other = product_t(low, w_in, bf16, 1 - tensor_index)
        arrived = pair_swap(other)
        low = after(low, other)
        if l > 0:
            grad_in = t_product(normed, low, bf16, 0, 2 * width)
            done_in = lax.psum_scatter(grad_in, "dp", scatter_dimension=0, tiled=True)
            low = after(low, grad_in)
            own = product_t(low, w_in, f32, tensor_index)
            done_out = lax.psum_scatter(grad_out, "dp", scatter_dimension=0, tiled=True)
            arrived, own, done_out = lax.optimization_barrier((arrived, own, done_out))
            out_parts[l] = done_out
            low_last, normed_last = low, normed
        else:
            in_state = []
            for i in range(2):
                part = t_product(normed, low, bf16, i * width, width)
                in_state.append(fold(row_blocks(part), 0)[0])
                low = after(low, part)
                if i == 0:
                    side = t_mm(normed, low[:, 2 * width :])
                    low = after(low, side)
            own = product_t(after(low, in_state), w_in, f32, tensor_index)
            for level in range(1, len(dp_factors()) - 1):
                in_state = [fold(q, level)[0] for q in in_state]
            arrived = after(arrived, in_state)
        normed_grad = own + arrived.astype(f32)
        unit = current * rms
        weighted = normed_grad * pre_gain[l][None, :]
        grad_pre = jnp.sum(other.astype(f32) * other_half(normed).astype(f32), axis=0)
        grad_pre = grad_pre + jnp.sum(own * own_half(normed).astype(f32), axis=0)
        grad_pre = grad_pre / pre_gain[l]
        grad_rows = grad_rows + rms * (
            weighted - unit * jnp.mean(weighted * unit, axis=1, keepdims=True)
        )
        gchan = gchan.at[7].set(grad_pre)
        packed[l] = jnp.concatenate([gchan, gbc, gdt], axis=1)
        if l > 0:
            low_last = after(low_last, grad_rows)
            side_last = t_mm(normed_last, low_last[:, 2 * width :])
    done_out = lax.psum_scatter(grad_out, "dp", scatter_dimension=0, tiled=True)
    side_width = 384
    side = jnp.concatenate([side, side_last], axis=1)
    side_own = lax.psum_scatter(side, "dp", scatter_dimension=0, tiled=True)
    small = jnp.stack(packed)
    row = lax.broadcasted_iota(jnp.int32, small.shape, 1)
    col = lax.broadcasted_iota(jnp.int32, small.shape, 2)
    shared = ((row == 7) & (col < width)) | ((col >= width) & (col < width + 256))
    small = small + jnp.where(shared, pair_swap(small), 0.0)
    spans = [1]
    while spans[-1] * 2 < lax.axis_size("dp"):
        spans.append(spans[-1] * 2)
    small = sum_devices(small, spans[:1] + spans[:1:-1])
    queue = in_state
    level = len(dp_factors()) - 1
    for n in range(len(queue)):
        marks = (small, small, side_own) if n == len(queue) - 1 else ()
        queue[n], _ = fold(queue[n], level, marks=marks)
    small = sum_devices(after(small, queue[0]), spans[1:2])
    done = [q.reshape(q.shape[1:]) for q in queue]
    out_parts[0] = done_out
    in_parts = [jnp.concatenate(done, axis=1), done_in]
    side_parts = [side_own[:, :side_width], side_own[:, side_width : 2 * side_width]]
    for l in range(layers):
        grad_bc = side_parts[l][:, :256]
        outputs[l] = (
            in_parts[l].astype(f32).reshape(-1, 2, width),
            grad_bc + pair_swap(grad_bc),
            side_parts[l][:, 256 : 256 + heads],
            out_parts[l].astype(f32).T,
        )
    grad_w_zx, grad_w_bc, grad_w_dt, grad_w_out = (
        jnp.stack([o[i] for o in outputs]) for i in range(4)
    )
    return (
        hidden_out,
        grad_rows,
        small[:, 7, :width],
        grad_w_zx,
        grad_w_bc,
        grad_w_dt,
        small[:, 0:4, :width],
        small[:, 4, :width],
        small[:, 0:4, width : width + 256],
        small[:, 4, width : width + 256],
        small[:, 0, width + 256 : width + 256 + heads],
        small[:, 1, width + 256 : width + 256 + heads],
        jnp.sum(small[:, 6, :width].reshape(layers, heads, HEADDIM), axis=2),
        small[:, 5, :width],
        grad_w_out,
    )


def solution(mesh):
    return jax.shard_map(
        local,
        mesh=mesh,
        in_specs=(
            P(("dp", "tensor"), None),
            P(),
            P(None, "dp", None, "tensor"),
            P(None, "dp", None),
            P(None, "dp", "tensor"),
            P(None, None, "tensor"),
            P(None, "tensor"),
            P(),
            P(),
            P(None, "tensor"),
            P(None, "tensor"),
            P(None, "tensor"),
            P(None, "tensor"),
            P(None, "tensor", "dp"),
            P(("dp", "tensor"), None),
        ),
        out_specs=(
            P(("dp", "tensor"), None),
            P(("dp", "tensor"), None),
            P(),
            P(None, "dp", None, "tensor"),
            P(None, "dp", None),
            P(None, "dp", "tensor"),
            P(None, None, "tensor"),
            P(None, "tensor"),
            P(),
            P(),
            P(None, "tensor"),
            P(None, "tensor"),
            P(None, "tensor"),
            P(None, "tensor"),
            P(None, "tensor", "dp"),
        ),
        check_vma=False,
    )
```

```python
import functools
import jax
import jax.numpy as jnp
from jax import lax
from jax.experimental import pallas as pl
from jax.experimental.pallas import tpu as pltpu
from jax.sharding import PartitionSpec as P

HEADDIM = 64
INNER = 3072
LANES = 128
Q = 128
GROUP = 256
LOG2E = 1.4426950408889634
epsilon = 1e-05
highest = lax.Precision.HIGHEST
bf16 = jnp.bfloat16
f32 = jnp.float32


def sigmoid(v):
    return 0.5 * jnp.tanh(0.5 * v) + 0.5


def mm(a, b, precision=None):
    return lax.dot_general(
        a, b, (((1,), (0,)), ((), ())), precision=precision, preferred_element_type=f32
    )


def mm_t(a, b):
    return lax.dot_general(a, b, (((1,), (1,)), ((), ())), preferred_element_type=f32)


def t_mm(a, b):
    return lax.dot_general(a, b, (((0,), (0,)), ((), ())), preferred_element_type=f32)


def iota2(shape, dim):
    return lax.broadcasted_iota(jnp.int32, shape, dim)


def split_lanes(v):
    high = v.astype(bf16).astype(f32)
    rest = v - high
    return (high + pltpu.roll(rest, 32, axis=1)).astype(bf16)


def taps_sum(ext_ref, taps_ref, bias_ref, columns):
    total = bias_ref[0:1, columns]
    for k in range(4):
        total = total + taps_ref[k : k + 1, columns] * ext_ref[5 + k : 5 + k + Q, columns]
    return total


def chunk_terms(bcdt_ref, bext_ref, bct_ref, bcb_ref, dtv_ref, head_count):
    bext_ref[8 : 8 + Q, :] = bcdt_ref[:, 0:256]
    z = taps_sum(bext_ref, bct_ref, bcb_ref, slice(0, 256))
    s = sigmoid(z)
    bc = z * s
    dsilu = s * (1.0 + z * (1.0 - s))
    b_part = bc[:, 0:128]
    c_part = bc[:, 128:256]
    pre = bcdt_ref[:, 256:384] + dtv_ref[0:1, :]
    live = iota2((Q, LANES), 1) < head_count
    step = jnp.where(live, jnp.maximum(pre, 0.0) + jnp.log1p(jnp.exp(-jnp.abs(pre))), 0.0)
    decay = step * dtv_ref[1:2, :]
    rows = iota2((Q, Q), 0)
    cols = iota2((Q, Q), 1)
    lower = rows >= cols
    cum = mm(lower.astype(f32), decay, highest)
    return b_part, c_part, dsilu, pre, live, step, decay, cum, lower


def fwd_kernel(
    zx_ref, bcdt_ref, taps_ref, chan_ref, bct_ref, bcb_ref, dtv_ref, spread_ref,
    sh_ref, mixed_ref, sin_ref, ssq_ref, ext_ref, bext_ref, state_ref, *, head_count,
):
    width = sh_ref.shape[1]

    @pl.when(pl.program_id(0) == 0)
    def _():
        ext_ref[0:8, :] = jnp.zeros((8, width), f32)
        bext_ref[0:8, :] = jnp.zeros((8, 256), f32)
        state_ref[...] = jnp.zeros_like(state_ref)

    @pl.when(pl.program_id(0) > 0)
    def _():
        ext_ref[0:8, :] = ext_ref[Q : Q + 8, :]
        bext_ref[0:8, :] = bext_ref[Q : Q + 8, :]

    b_part, c_part, _, _, live, step, decay, cum, lower = chunk_terms(
        bcdt_ref, bext_ref, bct_ref, bcb_ref, dtv_ref, head_count
    )
    cum2 = cum * LOG2E
    across = cum2.T
    last = cum2[Q - 1 : Q, :]
    bb = b_part.astype(bf16)
    cb = c_part.astype(bf16)
    bt = b_part.T.astype(bf16)
    c_both = jnp.concatenate([cb, (c_part - cb.astype(f32)).astype(bf16)], axis=1)
    scores = jnp.where(lower, mm(c_part, b_part.T, highest), 0.0)
    step_l = split_lanes(step)
    grow_l = split_lanes(jnp.where(live, jnp.exp2(cum2), 0.0))
    left_l = split_lanes(jnp.where(live, jnp.exp2(last - cum2), 0.0))
    all_l = split_lanes(jnp.where(live[0:16], jnp.exp2(jnp.broadcast_to(last, (16, LANES))), 0.0))
    stacked = jnp.concatenate([step_l, grow_l, left_l, all_l], axis=0)
    half = iota2((Q, LANES), 1) < HEADDIM
    ssq = jnp.zeros((Q, LANES), f32)
    for g in range(width // GROUP):
        columns = slice(g * GROUP, (g + 1) * GROUP)
        spread = spread_ref[:, columns]
        spreads = mm(stacked, spread)
        step_e = spreads[0:Q]
        grow_e = spreads[Q : 2 * Q]
        left_e = spreads[2 * Q : 3 * Q]
        all_e = spreads[3 * Q : 3 * Q + 1]
        ext_ref[8 : 8 + Q, columns] = zx_ref[:, width + g * GROUP : width + (g + 1) * GROUP].astype(f32)
        z = taps_sum(ext_ref, taps_ref, chan_ref, columns)
        xc = z * sigmoid(z)
        v = xc * step_e
        vb = v.astype(bf16)
        vl = (v - vb.astype(f32)).astype(bf16)
        state = state_ref[:, columns]
        state_b = state.astype(bf16)
        sin_ref[0, :, columns] = state
        state_l = (state - state_b.astype(f32)).astype(bf16)
        y = mm(c_both, jnp.concatenate([state_b, state_b], axis=0)) + mm(cb, state_l)
        y = y * grow_e
        parts = []
        for pair in range(GROUP // LANES):
            head = (g * GROUP + pair * LANES) // HEADDIM
            lanes = slice(pair * LANES, (pair + 1) * LANES)
            vp, vq = vb[:, lanes], vl[:, lanes]
            highs, lows = [], []
            for h in (head, head + 1):
                d = cum2[:, h : h + 1] - across[h : h + 1, :]
                m = scores * jnp.exp2(-jnp.abs(d))
                mb = m.astype(bf16)
                highs.append(mb)
                lows.append((m - mb.astype(f32)).astype(bf16))
            block = [jnp.where(half, vp, 0), jnp.where(half, 0, vp)]
            block_l = [jnp.where(half, vq, 0), jnp.where(half, 0, vq)]
            parts.append(
                mm(
                    jnp.concatenate(highs + lows + highs, axis=1),
                    jnp.concatenate(block + block + block_l, axis=0),
                )
            )
        y = y + jnp.concatenate(parts, axis=1)
        state_ref[:, columns] = state * all_e + mm(bt, (v * left_e).astype(bf16))
        mixed = y + chan_ref[2:3, columns] * xc
        mixed_ref[:, columns] = mixed
        gate = zx_ref[:, columns].astype(f32)
        gated = mixed * (gate * sigmoid(gate))
        squares = gated * gated
        ssq = ssq + squares[:, 0:LANES] + squares[:, LANES : 2 * LANES]
        sh_ref[:, columns] = gated * chan_ref[1:2, columns]
    ssq_ref[...] = ssq


def bwd_kernel(
    sg_ref, zx_ref, xprev_ref, mixed_ref, sin_ref, bcdt_ref, bcprev_ref, coef_ref,
    taps_ref, chan_ref, bct_ref, bcb_ref, dtv_ref, spread_ref, gather_ref,
    low_ref, gchan_ref, gbc_ref, gdt_ref,
    ext_ref, bext_ref, dz_ref, dbz_ref, dstate_ref, colsum_ref, *, head_count,
):
    width = sg_ref.shape[1]
    step_id = pl.program_id(0)
    is_first = step_id == pl.num_programs(0) - 1

    @pl.when(step_id == 0)
    def _():
        dz_ref[Q : Q + 8, :] = jnp.zeros((8, width), f32)
        dbz_ref[Q : Q + 8, :] = jnp.zeros((8, 256), f32)
        dstate_ref[...] = jnp.zeros_like(dstate_ref)
        gchan_ref[...] = jnp.zeros_like(gchan_ref)
        gbc_ref[...] = jnp.zeros_like(gbc_ref)
        gdt_ref[...] = jnp.zeros_like(gdt_ref)
        colsum_ref[...] = jnp.zeros_like(colsum_ref)

    @pl.when(step_id > 0)
    def _():
        dz_ref[Q : Q + 8, :] = dz_ref[0:8, :]
        dbz_ref[Q : Q + 8, :] = dbz_ref[0:8, :]

    keep = jnp.where(is_first, 0.0, 1.0)
    ext_ref[0:8, :] = xprev_ref[8:16, :].astype(f32) * keep
    bext_ref[0:8, :] = bcprev_ref[:, 0:256] * keep
    b_part, c_part, bc_dsilu, dt_pre, live, step, decay, cum, lower = chunk_terms(
        bcdt_ref, bext_ref, bct_ref, bcb_ref, dtv_ref, head_count
    )
    cum2 = cum * LOG2E
    across = cum2.T
    last = cum2[Q - 1 : Q, :]
    bb = b_part.astype(bf16)
    cb = c_part.astype(bf16)
    bt = b_part.T.astype(bf16)
    ct = c_part.T.astype(bf16)
    c_both = jnp.concatenate([cb, (c_part - cb.astype(f32)).astype(bf16)], axis=1)
    b_both = jnp.concatenate([bb, (b_part - bb.astype(f32)).astype(bf16)], axis=1)
    upper = iota2((Q, Q), 0) <= iota2((Q, Q), 1)
    scores = jnp.where(lower, mm(c_part, b_part.T, highest), 0.0)
    scores_t = scores.T
    step_l = split_lanes(step)
    grow_l = split_lanes(jnp.where(live, jnp.exp2(cum2), 0.0))
    left_l = split_lanes(jnp.where(live, jnp.exp2(last - cum2), 0.0))
    all_l = split_lanes(jnp.where(live[0:16], jnp.exp2(jnp.broadcast_to(last, (16, LANES))), 0.0))
    stacked = jnp.concatenate([step_l, grow_l, left_l, all_l], axis=0)
    half = iota2((Q, LANES), 1) < HEADDIM
    coef = coef_ref[:, 0:1]
    inv = coef_ref[:, 1:2]
    d_scores = jnp.zeros((Q, Q), f32)
    d_c = jnp.zeros((Q, LANES), f32)
    d_b = jnp.zeros((Q, LANES), f32)
    row_sums = jnp.zeros((Q, LANES), f32)
    reduced = jnp.zeros((3 * Q, LANES), f32)
    red_all = jnp.zeros((8, LANES), f32)
    ones = jnp.ones((16, Q), bf16)
    pair_rows = iota2((2 * Q, LANES), 0) // Q
    pair_cols = iota2((2 * Q, LANES), 1)
    for g in range(width // GROUP):
        columns = slice(g * GROUP, (g + 1) * GROUP)
        spread = spread_ref[:, columns]
        gather = gather_ref[columns, :]
        spreads = mm(stacked, spread)
        step_e = spreads[0:Q]
        grow_e = spreads[Q : 2 * Q]
        left_e = spreads[2 * Q : 3 * Q]
        all_e = spreads[3 * Q : 3 * Q + 1]
        ext_ref[8 : 8 + Q, columns] = zx_ref[:, width + g * GROUP : width + (g + 1) * GROUP].astype(f32)
        z = taps_sum(ext_ref, taps_ref, chan_ref, columns)
        s = sigmoid(z)
        xc = z * s
        x_dsilu = s * (1.0 + z * (1.0 - s))
        gate = zx_ref[:, columns].astype(f32)
        gs = sigmoid(gate)
        act = gate * gs
        act_d = gs * (1.0 + gate * (1.0 - gs))
        mixed = mixed_ref[:, columns].astype(f32)
        gated = mixed * act
        sg = sg_ref[:, columns] * inv
        grad_gated = sg * chan_ref[1:2, columns] - gated * coef
        dy = grad_gated * act
        low_ref[:, columns] = (grad_gated * mixed * act_d).astype(bf16)
        gchan_ref[5:6, columns] += jnp.sum(sg * gated, axis=0, keepdims=True)
        gchan_ref[6:7, columns] += jnp.sum(dy * xc, axis=0, keepdims=True)
        dyb = dy.astype(bf16)
        v = xc * step_e
        vb = v.astype(bf16)
        sin_full = sin_ref[0, :, columns]
        sin = sin_full.astype(bf16)
        ey = dy * grow_e
        eyb = ey.astype(bf16)
        inter = ey * mm(c_both, jnp.concatenate([sin, sin], axis=0))
        dstate = dstate_ref[:, columns]
        dstate_b = dstate.astype(bf16)
        dv_state = mm(b_both, jnp.concatenate([dstate_b, dstate_b], axis=0)) * left_e
        d_c = d_c + mm_t(eyb, sin)
        d_b = d_b + mm_t((v * left_e).astype(bf16), dstate_b)
        kept = jnp.sum(sin_full * dstate, axis=0, keepdims=True) * all_e
        dstate_ref[:, columns] = dstate * all_e + mm(ct, eyb)
        parts = []
        for pair in range(GROUP // LANES):
            lanes = slice(pair * LANES, (pair + 1) * LANES)
            head = (g * GROUP + pair * LANES) // HEADDIM
            vp = vb[:, lanes]
            dp = dyb[:, lanes]
            v_block = jnp.concatenate([jnp.where(half, vp, 0), jnp.where(half, 0, vp)], axis=0)
            d_block = jnp.concatenate([jnp.where(half, dp, 0), jnp.where(half, 0, dp)], axis=0)
            dm = mm_t(dp, v_block)
            mts = []
            ws = []
            for i, h in enumerate((head, head + 1)):
                d = cum2[:, h : h + 1] - across[h : h + 1, :]
                e = jnp.exp2(-jnp.abs(d))
                dme = dm[:, i * Q : (i + 1) * Q] * e
                d_scores = d_scores + dme
                mts.append((scores_t * e).astype(bf16))
                ws.append((dme * scores).astype(bf16))
            parts.append(mm(jnp.concatenate(mts, axis=1), d_block))
            w = jnp.concatenate(ws, axis=1)
            picks = (pair_cols == head + pair_rows).astype(bf16)
            row_sums = row_sums + mm(w, picks)
            sums = mm(ones, w)
            colsum_ref[head : head + 1, :] = sums[0:1, 0:Q]
            colsum_ref[head + 1 : head + 2, :] = sums[0:1, Q : 2 * Q]
        dv = jnp.concatenate(parts, axis=1) + dv_state
        terms = jnp.concatenate([dv * xc, inter, v * dv_state], axis=0)
        terms_b = terms.astype(bf16)
        terms_l = (terms - terms_b.astype(f32)).astype(bf16)
        reduced = reduced + mm(terms_b, gather) + mm(terms_l, gather)
        red_all = red_all + mm(jnp.broadcast_to(kept, (8, GROUP)), gather.astype(f32), highest)
        dz = (dv * step_e + chan_ref[2:3, columns] * dy) * x_dsilu
        dz_ref[0:Q, columns] = dz
        dx = jnp.zeros((Q, GROUP), f32)
        for k in range(4):
            dx = dx + taps_ref[k : k + 1, columns] * dz_ref[3 - k : 3 - k + Q, columns]
            gchan_ref[k : k + 1, columns] += jnp.sum(
                dz * ext_ref[5 + k : 5 + k + Q, columns], axis=0, keepdims=True
            )
        gchan_ref[4:5, columns] += jnp.sum(dz, axis=0, keepdims=True)
        low_ref[:, width + g * GROUP : width + (g + 1) * GROUP] = dx.astype(bf16)
    red_step = reduced[0:Q]
    red_in = reduced[Q : 2 * Q]
    red_out = reduced[2 * Q : 3 * Q]
    through = row_sums - colsum_ref[...].T + red_in
    d_decay = mm(upper.astype(f32), through, highest) + mm(
        jnp.where(upper, 0.0, 1.0), red_out, highest
    ) + red_all[0:1, :]
    d_decay = jnp.where(live, d_decay, 0.0)
    d_pre = (red_step + d_decay * dtv_ref[1:2, :]) * sigmoid(dt_pre)
    d_pre = jnp.where(live, d_pre, 0.0)
    gdt_ref[0:1, :] += jnp.sum(d_pre, axis=0, keepdims=True)
    gdt_ref[1:2, :] += jnp.sum(d_decay * decay, axis=0, keepdims=True)
    low_ref[:, 2 * width + 256 : 2 * width + 384] = d_pre.astype(bf16)
    d_scores = jnp.where(lower, d_scores, 0.0)
    d_c = d_c + mm(d_scores, b_part, highest)
    d_b = d_b + mm(d_scores.T, c_part, highest)
    dbz = jnp.concatenate([d_b, d_c], axis=1) * bc_dsilu
    dbz_ref[0:Q, :] = dbz
    dbc = jnp.zeros((Q, 256), f32)
    for k in range(4):
        dbc = dbc + bct_ref[k : k + 1, :] * dbz_ref[3 - k : 3 - k + Q, :]
        gbc_ref[k : k + 1, :] += jnp.sum(
            dbz * bext_ref[5 + k : 5 + k + Q, :], axis=0, keepdims=True
        )
    gbc_ref[4:5, :] += jnp.sum(dbz, axis=0, keepdims=True)
    low_ref[:, 2 * width : 2 * width + 256] = dbc.astype(bf16)


def spread_matrix(width):
    heads = jnp.arange(width) // HEADDIM
    lanes = jnp.arange(LANES)
    return ((lanes[:, None] == heads[None, :]) | (lanes[:, None] == heads[None, :] + 32)).astype(bf16)


def gather_matrix(width):
    heads = jnp.arange(width) // HEADDIM
    return (heads[:, None] == jnp.arange(LANES)[None, :]).astype(bf16)


def whole(shape):
    return pl.BlockSpec(shape, lambda c: (0,) * len(shape))


VMEM_LIMIT = 48 * 1024 * 1024
LIGHT = pl.CostEstimate(flops=1000, bytes_accessed=1000, transcendentals=0)


def product_t(a, b, out_dtype, half, columns=512):
    rows = a.shape[0] // 2
    count, depth = b.shape

    def body(half_ref, a_ref, b_ref, o_ref):
        o_ref[...] = mm_t(a_ref[...], b_ref[...]).astype(out_dtype)

    return pl.pallas_call(
        body,
        grid_spec=pltpu.PrefetchScalarGridSpec(
            num_scalar_prefetch=1,
            grid=(count // columns,),
            in_specs=[
                pl.BlockSpec((rows, depth), lambda j, h: (h[0], 0)),
                pl.BlockSpec((columns, depth), lambda j, h: (j, 0)),
            ],
            out_specs=pl.BlockSpec((rows, columns), lambda j, h: (0, j)),
        ),
        out_shape=jax.ShapeDtypeStruct((rows, count), out_dtype),
        compiler_params=pltpu.CompilerParams(vmem_limit_bytes=VMEM_LIMIT),
        cost_estimate=LIGHT,
    )(half.reshape(1), a, b)


def t_product(a, b, out_dtype, first, count, columns=512):
    depth, rows = a.shape
    offset = first // columns

    def body(a_ref, b_ref, o_ref):
        o_ref[...] = t_mm(a_ref[...], b_ref[...]).astype(out_dtype)

    return pl.pallas_call(
        body,
        grid=(count // columns,),
        in_specs=[
            pl.BlockSpec((depth, rows), lambda j: (0, 0)),
            pl.BlockSpec((depth, columns), lambda j: (0, offset + j)),
        ],
        out_specs=pl.BlockSpec((rows, columns), lambda j: (0, j)),
        out_shape=jax.ShapeDtypeStruct((rows, count), out_dtype),
        compiler_params=pltpu.CompilerParams(vmem_limit_bytes=VMEM_LIMIT),
        cost_estimate=LIGHT,
    )(a, b)


def mixer_forward(zx, taps, chan, bct, bcb, dtv):
    rows = zx.shape[0]
    width2 = zx.shape[1] - 384
    width = width2 // 2
    side = width2 // 384
    chunks = rows // Q
    return pl.pallas_call(
        functools.partial(fwd_kernel, head_count=width // HEADDIM),
        grid=(chunks,),
        in_specs=[
            pl.BlockSpec((Q, width2), lambda c: (c, 0)),
            pl.BlockSpec((Q, 384), lambda c: (c, side)),
            whole((4, width)), whole((8, width)), whole((4, 256)), whole((1, 256)),
            whole((8, LANES)), whole((LANES, width)),
        ],
        out_specs=[
            pl.BlockSpec((Q, width), lambda c: (c, 0)),
            pl.BlockSpec((Q, width), lambda c: (c, 0)),
            pl.BlockSpec((1, LANES, width), lambda c: (c, 0, 0)),
            pl.BlockSpec((Q, LANES), lambda c: (c, 0)),
        ],
        out_shape=[
            jax.ShapeDtypeStruct((rows, width), f32),
            jax.ShapeDtypeStruct((rows, width), f32),
            jax.ShapeDtypeStruct((chunks, LANES, width), f32),
            jax.ShapeDtypeStruct((rows, LANES), f32),
        ],
        scratch_shapes=[
            pltpu.VMEM((Q + 8, width), f32),
            pltpu.VMEM((Q + 8, 256), f32),
            pltpu.VMEM((LANES, width), f32),
        ],
        compiler_params=pltpu.CompilerParams(
            dimension_semantics=("arbitrary",), vmem_limit_bytes=VMEM_LIMIT
        ),
        cost_estimate=LIGHT,
    )(zx, zx, taps, chan, bct, bcb, dtv, spread_matrix(width))


def mixer_backward(sg, zx, mixed, sin, coef, taps, chan, bct, bcb, dtv):
    rows = zx.shape[0]
    width2 = zx.shape[1] - 384
    width = width2 // 2
    side = width2 // 384
    chunks = rows // Q
    last = chunks - 1
    return pl.pallas_call(
        functools.partial(bwd_kernel, head_count=width // HEADDIM),
        grid=(chunks,),
        in_specs=[
            pl.BlockSpec((Q, width), lambda c: (last - c, 0)),
            pl.BlockSpec((Q, width2), lambda c: (last - c, 0)),
            pl.BlockSpec((16, width), lambda c: (jnp.maximum((last - c) * (Q // 16) - 1, 0), 1)),
            pl.BlockSpec((Q, width), lambda c: (last - c, 0)),
            pl.BlockSpec((1, LANES, width), lambda c: (last - c, 0, 0)),
            pl.BlockSpec((Q, 384), lambda c: (last - c, side)),
            pl.BlockSpec((8, 384), lambda c: (jnp.maximum((last - c) * (Q // 8) - 1, 0), side)),
            pl.BlockSpec((Q, LANES), lambda c: (last - c, 0)),
            whole((4, width)), whole((8, width)), whole((4, 256)), whole((1, 256)),
            whole((8, LANES)), whole((LANES, width)), whole((width, LANES)),
        ],
        out_specs=[
            pl.BlockSpec((Q, width2 + 384), lambda c: (last - c, 0)),
            whole((8, width)), whole((8, 256)), whole((8, LANES)),
        ],
        out_shape=[
            jax.ShapeDtypeStruct((rows, width2 + 384), bf16),
            jax.ShapeDtypeStruct((8, width), f32),
            jax.ShapeDtypeStruct((8, 256), f32),
            jax.ShapeDtypeStruct((8, LANES), f32),
        ],
        scratch_shapes=[
            pltpu.VMEM((Q + 8, width), f32),
            pltpu.VMEM((Q + 8, 256), f32),
            pltpu.VMEM((Q + 8, width), f32),
            pltpu.VMEM((Q + 8, 256), f32),
            pltpu.VMEM((LANES, width), f32),
            pltpu.VMEM((LANES, LANES), f32),
        ],
        compiler_params=pltpu.CompilerParams(
            dimension_semantics=("arbitrary",), vmem_limit_bytes=VMEM_LIMIT
        ),
        cost_estimate=LIGHT,
    )(sg, zx, zx, mixed, sin, zx, zx, coef, taps, chan, bct, bcb, dtv,
      spread_matrix(width), gather_matrix(width))


def pair_swap(v):
    return lax.ppermute(v, "tensor", ((0, 1), (1, 0)))


def both_rows(own, other, first):
    return jnp.where(
        first, jnp.concatenate([own, other], axis=0), jnp.concatenate([other, own], axis=0)
    )


def dp_factors():
    size = lax.axis_size("dp")
    known = {16: (2, 2, 4), 64: (2, 4, 2, 4)}
    return known.get(size, (size,))


def after(v, other):
    return lax.optimization_barrier((v, other))[0]


def row_blocks(v):
    size = lax.axis_size("dp")
    return v.reshape((size, v.shape[0] // size) + v.shape[1:])


def fold(blocks, level, gate=None):
    factors = dp_factors()
    factor = factors[level]
    stride = 1
    for f in factors[:level]:
        stride *= f
    size = lax.axis_size("dp")
    place = (lax.axis_index("dp") // stride) % factor
    hops = []
    for i in range(size):
        here = (i // stride) % factor
        hops.append((i, i + ((here + 1) % factor - here) * stride))
    parts = blocks.reshape((blocks.shape[0] // factor, factor) + blocks.shape[1:])

    def pick(step):
        return lax.dynamic_index_in_dim(parts, (place + step) % factor, 1, keepdims=False)

    moving = pick(factor - 1)
    seen = []
    for step in range(factor - 1):
        if gate is not None and step == factor - 2:
            moving = after(moving, gate(seen))
        arrived = lax.ppermute(moving, "dp", hops)
        seen.append(arrived)
        moving = (arrived.astype(f32) + pick(2 * factor - 2 - step).astype(f32)).astype(blocks.dtype)
    return moving


def sum_devices(v, spans):
    size = lax.axis_size("dp")
    for span in spans:
        v = v + lax.ppermute(v, "dp", [(i, i ^ span) for i in range(size)])
    return v


def head_lanes(v):
    return jnp.pad(v, ((0, LANES - v.shape[0]),))


def local(
    hidden,
    pre_gain,
    w_zx,
    w_bc,
    w_dt,
    conv_x,
    conv_x_bias,
    conv_bc,
    conv_bc_bias,
    dt_bias,
    a_log,
    d_skip,
    norm_gain,
    w_out,
    cotangent,
):
    layers = pre_gain.shape[0]
    own_count, depth = hidden.shape
    rows = own_count * lax.axis_size("tensor")
    width = w_zx.shape[-1]
    heads = dt_bias.shape[-1]
    tensor_index = lax.axis_index("tensor")
    first = tensor_index == 0

    def own_half(v):
        return lax.dynamic_slice_in_dim(v, tensor_index * own_count, own_count, 0)

    def other_half(v):
        return lax.dynamic_slice_in_dim(v, (1 - tensor_index) * own_count, own_count, 0)

    def gather_pair(v):
        return both_rows(v, pair_swap(v), first)

    in_weights = []
    out_weights = []
    for l in range(layers):
        shard = jnp.concatenate(
            [
                w_zx[l].reshape(w_zx.shape[1], -1),
                w_bc[l],
                jnp.pad(w_dt[l], ((0, 0), (0, LANES - heads))),
            ],
            axis=1,
        )
        out_shard = w_out[l].T
        in_weights.append(lax.all_gather(shard, "dp", axis=0, tiled=True))
        out_weights.append(lax.all_gather(out_shard, "dp", axis=0, tiled=True))
    params = []
    for l in range(layers):
        chan = jnp.zeros((8, width), f32)
        chan = chan.at[0].set(conv_x_bias[l]).at[1].set(norm_gain[l])
        chan = chan.at[2].set(jnp.repeat(d_skip[l], HEADDIM))
        dtv = jnp.zeros((8, LANES), f32)
        dtv = dtv.at[0].set(head_lanes(dt_bias[l])).at[1].set(head_lanes(-jnp.exp(a_log[l])))
        params.append((conv_x[l], chan, conv_bc[l], conv_bc_bias[l][None, :], dtv))

    current = hidden.astype(f32)
    saved = []
    for l in range(layers):
        w_in = in_weights[l]
        rms = lax.rsqrt(jnp.mean(current * current, axis=1, keepdims=True) + epsilon)
        own_normed = (current * rms * pre_gain[l][None, :]).astype(bf16)
        if l == 0:
            arrived = pair_swap(jnp.concatenate([own_normed, cotangent], axis=0))
            normed = both_rows(own_normed, arrived[:own_count], first)
            cot = both_rows(cotangent, arrived[own_count:], first)
        else:
            normed = gather_pair(own_normed)
        zx = mm(normed, w_in)
        scaled, mixed, states, squares = mixer_forward(zx, *params[l])
        squares = jnp.sum(squares, axis=1).reshape(8, -1)
        squares = (squares + pair_swap(squares)).reshape(rows, 1)
        inv = lax.rsqrt(squares / INNER + epsilon)
        shaped = (scaled * inv).astype(bf16)
        other = mm_t(other_half(shaped), out_weights[l])
        own = mm_t(own_half(shaped), out_weights[l])
        outgoing = other.astype(bf16)
        if l == layers - 1:
            own_dot = jnp.sum(own_half(cot).astype(f32) * own, axis=1, keepdims=True)
            other_dot = jnp.sum(other_half(cot).astype(f32) * other, axis=1, keepdims=True)
            dots = jnp.where(
                first,
                jnp.concatenate([own_dot, other_dot], axis=0),
                jnp.concatenate([other_dot, own_dot], axis=0),
            ).reshape(8, -1)
            dots = dots + pair_swap(dots)
            last_dot = dots.reshape(rows, 1)
            arrived = pair_swap(after(outgoing, dots))
            last_own, last_arrived = own, arrived
        else:
            arrived = pair_swap(outgoing)
        lifted = own + arrived.astype(f32)
        saved.append((current, rms, normed, zx, shaped, mixed, states, inv, lifted))
        if l < layers - 1:
            current = current + lifted
    grad_rows = cotangent.astype(f32)
    outputs = [None] * layers
    out_parts = [None] * layers
    packed = [None] * layers
    for l in reversed(range(layers)):
        current, rms, normed, zx, shaped, mixed, states, inv, lifted = saved[l]
        w_in = in_weights[l]
        if l == layers - 1:
            out_grad = cot
            row_dot = last_dot
        else:
            own_grad = grad_rows.astype(bf16)
            out_grad, side_last = lax.optimization_barrier((gather_pair(own_grad), side_last))
            own_dot = jnp.sum(own_grad.astype(f32) * lifted, axis=1).reshape(8, -1)
            row_dot = both_rows(own_dot.reshape(-1, 1), pair_swap(own_dot).reshape(-1, 1), first)
        coef = jnp.pad(
            jnp.concatenate([inv * inv * row_dot / INNER, inv], axis=1), ((0, 0), (0, LANES - 2))
        )
        shaped_grad = mm(out_grad, out_weights[l])
        grad_out = t_mm(out_grad, shaped).astype(bf16)
        low, gchan, gbc, gdt = mixer_backward(
            shaped_grad, zx, mixed, states, coef, *params[l]
        )
        if l == layers - 1:
            low, last_arrived = lax.optimization_barrier((low, last_arrived))
            hidden_out = saved[l][0] + last_own + last_arrived.astype(f32)
        if l == 0:
            low, done_in = lax.optimization_barrier((low, done_in))
        other = product_t(low, w_in, bf16, 1 - tensor_index)
        arrived = pair_swap(other)
        low = after(low, other)
        if l > 0:
            grad_in = t_product(normed, low, bf16, 0, 2 * width)
            done_in = lax.psum_scatter(grad_in, "dp", scatter_dimension=0, tiled=True)
            low = after(low, grad_in)
            own = product_t(low, w_in, f32, tensor_index)
            done_out = lax.psum_scatter(grad_out, "dp", scatter_dimension=0, tiled=True)
            arrived, own, done_out = lax.optimization_barrier((arrived, own, done_out))
            out_parts[l] = done_out
            low_last, normed_last = low, normed
        else:
            side = t_mm(normed, low[:, 2 * width :])
            side = lax.dynamic_update_slice(side_last, side, (0, 0))
            low = after(low, side)
            in_state = []
            for i in range(2):
                part = t_product(normed, low, bf16, i * width, width)
                in_state.append(fold(row_blocks(part), 0))
                low = after(low, part)
            own = product_t(after(low, in_state), w_in, f32, tensor_index)
            for level in range(1, len(dp_factors()) - 1):
                in_state = [fold(q, level) for q in in_state]
            arrived = after(arrived, in_state)
        normed_grad = own + arrived.astype(f32)
        unit = current * rms
        weighted = normed_grad * pre_gain[l][None, :]
        grad_pre = jnp.sum(other.astype(f32) * other_half(normed).astype(f32), axis=0)
        grad_pre = grad_pre + jnp.sum(own * own_half(normed).astype(f32), axis=0)
        grad_pre = grad_pre / pre_gain[l]
        grad_rows = grad_rows + rms * (
            weighted - unit * jnp.mean(weighted * unit, axis=1, keepdims=True)
        )
        gchan = gchan.at[7].set(grad_pre)
        packed[l] = jnp.concatenate([gchan, gbc, gdt], axis=1)
        if l > 0:
            low_last = after(low_last, grad_rows)
            side_last = t_mm(normed_last, low_last[:, 2 * width :])
            side_last = jnp.pad(side_last, ((0, 0), (side_last.shape[1], 0)))
    done_out = lax.psum_scatter(grad_out, "dp", scatter_dimension=0, tiled=True)
    side_width = 384
    side_own = lax.psum_scatter(side, "dp", scatter_dimension=0, tiled=True)
    small = jnp.stack(packed)
    row = lax.broadcasted_iota(jnp.int32, small.shape, 1)
    col = lax.broadcasted_iota(jnp.int32, small.shape, 2)
    shared = ((row == 7) & (col < width)) | ((col >= width) & (col < width + 256))
    small = small + jnp.where(shared, pair_swap(small), 0.0)
    spans = [1]
    while spans[-1] * 2 < lax.axis_size("dp"):
        spans.append(spans[-1] * 2)
    queue = in_state
    level = len(dp_factors()) - 1
    partial_sums = []

    def gate(seen):
        early = after(small, seen[0]) if seen else small
        partial_sums.append(sum_devices(early, spans[:1] + spans[:1:-1]))
        return partial_sums[0], side_own

    queue[0] = fold(queue[0], level)
    queue[1] = fold(queue[1], level, gate)
    small = sum_devices(after(partial_sums[0], queue[0]), spans[1:2])
    done = [q.reshape(q.shape[1:]) for q in queue]
    out_parts[0] = done_out
    in_parts = [jnp.concatenate(done, axis=1), done_in]
    side_parts = [side_own[:, :side_width], side_own[:, side_width : 2 * side_width]]
    for l in range(layers):
        grad_bc = side_parts[l][:, :256]
        outputs[l] = (
            in_parts[l].astype(f32).reshape(-1, 2, width),
            grad_bc + pair_swap(grad_bc),
            side_parts[l][:, 256 : 256 + heads],
            out_parts[l].astype(f32).T,
        )
    grad_w_zx, grad_w_bc, grad_w_dt, grad_w_out = (
        jnp.stack([o[i] for o in outputs]) for i in range(4)
    )
    return (
        hidden_out,
        grad_rows,
        small[:, 7, :width],
        grad_w_zx,
        grad_w_bc,
        grad_w_dt,
        small[:, 0:4, :width],
        small[:, 4, :width],
        small[:, 0:4, width : width + 256],
        small[:, 4, width : width + 256],
        small[:, 0, width + 256 : width + 256 + heads],
        small[:, 1, width + 256 : width + 256 + heads],
        jnp.sum(small[:, 6, :width].reshape(layers, heads, HEADDIM), axis=2),
        small[:, 5, :width],
        grad_w_out,
    )


def solution(mesh):
    return jax.shard_map(
        local,
        mesh=mesh,
        in_specs=(
            P(("dp", "tensor"), None),
            P(),
            P(None, "dp", None, "tensor"),
            P(None, "dp", None),
            P(None, "dp", "tensor"),
            P(None, None, "tensor"),
            P(None, "tensor"),
            P(),
            P(),
            P(None, "tensor"),
            P(None, "tensor"),
            P(None, "tensor"),
            P(None, "tensor"),
            P(None, "tensor", "dp"),
            P(("dp", "tensor"), None),
        ),
        out_specs=(
            P(("dp", "tensor"), None),
            P(("dp", "tensor"), None),
            P(),
            P(None, "dp", None, "tensor"),
            P(None, "dp", None),
            P(None, "dp", "tensor"),
            P(None, None, "tensor"),
            P(None, "tensor"),
            P(),
            P(),
            P(None, "tensor"),
            P(None, "tensor"),
            P(None, "tensor"),
            P(None, "tensor"),
            P(None, "tensor", "dp"),
        ),
        check_vma=False,
    )
```
